256 devices in a mesh: region: 8 (over x, core), member: 32 (over z, y).
Axes of the slice: x: 4, y: 4, z: 8, core: 2. Of those that a mesh axis runs over, the one named last changes fastest.
Arguments:
- background_trajectories: bfloat16 [256, 6, 65536], P('member', None, 'region'), may hold values from -6 to 6
- sensor_spread_matrix: bfloat16 [256, 114688], P('member', 'region'), may hold values from -2 to 2
- departure_vector: float32 [114688], P('region'), may hold values from -6 to 6
- inverse_error_variance: float32 [114688], P('region'), may hold values from 0.3 to 3
- edge_tile_handoff: int32 [2, 32], P(None, 'region'), may hold values from 0 to 55
- measurement_tile_table: int32 [512, 16], P(('region', 'member')), may hold values from 0 to 63
- distance_damping: float32 [512, 16], P(('region', 'member')), may hold values from 0.1 to 1
- active_tile_tally: int32 [512], P(('region', 'member')), may hold values from 1 to 16, as said below
Outputs:
- analysis: bfloat16 [256, 6, 65536], P('member', None, 'region')
The draws below stay inside these ranges and needn't reach their ends.
Inputs may be any that keep to these rules, and one draw needn't show every extreme that they name: `edge_tile_handoff`: indices of a region's own observation blocks. `measurement_tile_table`: indices into the region's extended set; entries at positions at or past active_tile_tally are unused. `active_tile_tally`: some column block uses all 16 slots.
All inputs are finite; a program needn't handle non-finite values. Where the reference program divides by a largest or mean magnitude, that divisor is 1e-20 or more.
Results may differ from the reference program's by a relative error of at most 0.0075.
Values may be sent and summed in bfloat16 or wider, within the bound.
No kernel may reach another device: no remote copies, remote signals or barrier semaphores. Data moves between devices by JAX's collectives and lax.ppermute only.
A program may use at most 128 MiB of HBM per device.

```python
import math
import jax
import jax.numpy as jnp
from jax import lax

MEMBERSHIP = 256
HEIGHT_STRATA = 6
READINGS_BUNDLE = 256
HB = 4
COMMON_STENCIL = 128
MAXL = 16
NSIT = 3
NEXT = 64
HOME_BUNDLES = 56
DOMAIN_STRIPS = 64
NCB = 512
PLANET_SITES = 65536
NOBS = 114688
N_REGION = 8


def draw_active_tile_tally(key, part):
    key = jax.random.fold_in(key, 11)
    first_key, second_key, place_key = jax.random.split(key, 3)
    first = jax.random.randint(first_key, (NCB,), 0, MAXL)
    second = jax.random.randint(second_key, (NCB,), 0, MAXL)
    counts = 1 + (first + second) // 2
    where = jax.random.randint(place_key, (), 0, NCB)
    return counts.at[where].set(MAXL).astype(jnp.int32)


def touch_ends(values, own_key, least, high):
    longest = values.shape.index(max(values.shape))
    spots = []
    for shift in (0, 1):
        where = [jax.random.randint(jax.random.fold_in(own_key, axis), (), 0, length) for axis, length in enumerate(values.shape)]
        where[longest] = (where[longest] + shift) % values.shape[longest]
        spots.append(tuple(where))
    return values.at[spots[0]].set(least).at[spots[1]].set(high)


def block_levels(rng, shape, shards, low, largest):
    def one(dim, shards_of):
        draws = jax.random.uniform(jax.random.fold_in(jax.random.fold_in(rng, 6), dim), (shards_of,), jnp.float32, low / len(shards), largest / len(shards))
        return jnp.repeat(jnp.exp(draws), shape[dim] // shards_of).reshape((-1,) + (1,) * (len(shape) - dim - 1))

    loudness = one(*shards[0])
    for cut in shards[1:]:
        loudness = loudness * one(*cut)
    return loudness


def scatter_about(stream_key, extent, spread, limit, cuts=(), kind=jnp.bfloat16):
    values = jax.random.normal(stream_key, extent, jnp.float32) * spread
    if len(cuts) > 0:
        values = block_levels(stream_key, extent, cuts, -0.22, 0.18) * values
    return jnp.clip(values, min=-limit, max=limit).astype(kind)


def setup_inputs(seed: int = 0) -> dict:
    streams_of = jax.random.split(jax.random.key(seed), 9)
    return {
        "background_trajectories": scatter_about(streams_of[0], (MEMBERSHIP, HEIGHT_STRATA, PLANET_SITES), 1.0, 6.0, ((0, 32), (2, 8))),
        "sensor_spread_matrix": scatter_about(streams_of[1], (MEMBERSHIP, NOBS), 0.3, 2.0, ((0, 32), (1, 8))),
        "departure_vector": scatter_about(streams_of[2], (NOBS,), 1.0, 6.0, ((0, 8),), jnp.float32),
        "inverse_error_variance": jnp.clip(jnp.exp(math.log(3.0) - 2.3025851 * jax.random.uniform(streams_of[3], (NOBS,), jnp.float32) ** block_levels(streams_of[3], (NOBS,), ((0, 8),), -0.2, 0.2)), 0.3, 3.0),
        "edge_tile_handoff": touch_ends(jax.random.randint(streams_of[4], (2, N_REGION * HB), 0, HOME_BUNDLES), jax.random.fold_in(streams_of[4], 1), 0, HOME_BUNDLES - 1).astype(jnp.int32),
        "measurement_tile_table": touch_ends(jax.random.randint(streams_of[5], (NCB, MAXL), 0, NEXT), jax.random.fold_in(streams_of[5], 1), 0, NEXT - 1).astype(jnp.int32),
        "distance_damping": jnp.clip(0.1 + 0.9 * jax.random.uniform(streams_of[6], (NCB, MAXL), jnp.float32) ** block_levels(streams_of[6], (NCB, MAXL), ((0, 256),), -0.2, 0.2), 0.1, 1.0),
        "active_tile_tally": draw_active_tile_tally(jax.random.fold_in(streams_of[8], 71), 0),
    }


def shift_down(array):
    return jnp.concatenate([jnp.zeros_like(array[:1]), array[:-1]], axis=0)

def shift_up(array):
    return jnp.concatenate([array[1:], jnp.zeros_like(array[:1])], axis=0)

def update_coefficients(cross_product_accumulated, projected_innovation, background_copies):
    unit_diagonal = jnp.eye(background_copies, dtype=jnp.float32)
    linear_equations = unit_diagonal + cross_product_accumulated / (background_copies - 1.0)
    bound = lax.optimization_barrier(jnp.max(lax.optimization_barrier(jnp.sum(jnp.abs(linear_equations), axis=-1)), axis=-1))
    root_iter = linear_equations / bound[:, None, None]
    inverse_root = jnp.broadcast_to(unit_diagonal, linear_equations.shape)
    for iteration in range(NSIT):
        factor = 1.5 * unit_diagonal - 0.5 * jnp.matmul(inverse_root, root_iter, precision=lax.Precision.HIGHEST)
        root_iter = jnp.matmul(root_iter, factor, precision=lax.Precision.HIGHEST)
        inverse_root = jnp.matmul(factor, inverse_root, precision=lax.Precision.HIGHEST)
    dispersion_factor = inverse_root / jnp.sqrt(bound)[:, None, None]
    scalar_product = jnp.matmul(dispersion_factor, projected_innovation[:, :, None], precision=lax.Precision.HIGHEST)
    centre_increment = jnp.matmul(dispersion_factor, scalar_product, precision=lax.Precision.HIGHEST)[:, :, 0] / (background_copies - 1.0)
    return (dispersion_factor + centre_increment[:, :, None]).astype(jnp.bfloat16)

def reference(background_trajectories, sensor_spread_matrix, departure_vector, inverse_error_variance, edge_tile_handoff, measurement_tile_table, distance_damping, active_tile_tally):
    background_copies = background_trajectories.shape[0]
    trajectory_family = sensor_spread_matrix.reshape(background_copies, N_REGION, HOME_BUNDLES, READINGS_BUNDLE).transpose(1, 0, 2, 3)
    values = departure_vector.reshape(N_REGION, HOME_BUNDLES, READINGS_BUNDLE)
    weights = inverse_error_variance.reshape(N_REGION, HOME_BUNDLES, READINGS_BUNDLE)
    picks = edge_tile_handoff.reshape(2, N_REGION, HB)
    take_ens = jax.vmap(lambda block_set, chosen: jnp.take(block_set, chosen, axis=1))
    take_obs = jax.vmap(lambda block_set, chosen: jnp.take(block_set, chosen, axis=0))
    ext_ens = jnp.concatenate([shift_down(take_ens(trajectory_family, picks[0])), trajectory_family, shift_up(take_ens(trajectory_family, picks[1]))], axis=2)
    ext_val = jnp.concatenate([shift_down(take_obs(values, picks[0])), values, shift_up(take_obs(values, picks[1]))], axis=1)
    ext_wgt = jnp.concatenate([shift_down(take_obs(weights, picks[0])), weights, shift_up(take_obs(weights, picks[1]))], axis=1)
    lists = measurement_tile_table.reshape(N_REGION, DOMAIN_STRIPS, MAXL)
    locs = distance_damping.reshape(N_REGION, DOMAIN_STRIPS, MAXL)
    counts = active_tile_tally.reshape(N_REGION, DOMAIN_STRIPS)
    atmospheric_quantities = background_trajectories.reshape(background_copies, HEIGHT_STRATA, N_REGION, DOMAIN_STRIPS, COMMON_STENCIL).transpose(2, 0, 1, 3, 4)

    def region_step(pieces):
        ens_reg, val_reg, wgt_reg, list_reg, loc_reg, count_reg, slab_portion = pieces
        ens_wide = ens_reg.astype(jnp.float32)
        scaled = (ens_wide * wgt_reg[None]).astype(jnp.bfloat16)
        scaled = lax.optimization_barrier(scaled).astype(jnp.float32)
        grams = jnp.einsum('ibo,jbo->bij', ens_wide, scaled, precision=lax.Precision.HIGHEST)
        vectors = jnp.einsum('ibo,bo->bi', ens_wide, wgt_reg * val_reg, precision=lax.Precision.HIGHEST)
        live = (jnp.arange(MAXL)[None, :] < count_reg[:, None]).astype(jnp.float32) * loc_reg
        match = (list_reg[:, :, None] == jnp.arange(NEXT, dtype=jnp.int32)[None, None, :]).astype(jnp.float32)
        coeffs = lax.optimization_barrier(jnp.sum(match * live[:, :, None], axis=1))
        cross_product_accumulated = jnp.einsum('cb,bij->cij', coeffs, grams, precision=lax.Precision.HIGHEST)
        projected_innovation = jnp.einsum('cb,bi->ci', coeffs, vectors, precision=lax.Precision.HIGHEST)
        combination_matrix = update_coefficients(cross_product_accumulated, projected_innovation, background_copies)
        average_centre = lax.optimization_barrier(jnp.sum(slab_portion.astype(jnp.float32), axis=0)) / background_copies
        pert = (slab_portion.astype(jnp.float32) - average_centre).astype(jnp.bfloat16)
        mixed = jnp.einsum('ilcq,cij->jlcq', pert.astype(jnp.float32), combination_matrix.astype(jnp.float32), precision=lax.Precision.HIGHEST)
        return (average_centre + mixed).astype(jnp.bfloat16)
    updated_estimate = lax.map(region_step, (ext_ens, ext_val, ext_wgt, lists, locs, counts, atmospheric_quantities))
    return updated_estimate.transpose(1, 2, 0, 3, 4).reshape(background_copies, HEIGHT_STRATA, PLANET_SITES)
```

```python
import jax
import jax.numpy as jnp
from jax import lax
from jax.experimental import pallas as pl
from jax.experimental.pallas import tpu as pltpu
from jax.sharding import PartitionSpec as P

F32 = jnp.float32
BF16 = jnp.bfloat16
MEMBERS = 256
PEERS = 32
OWN = 8
LEVELS = 6
OBS = 256
HANDED = 4
HOME = 56
EXT = 64
COLS = 256
MAXL = 16
VMEM_BYTES = 48 * 1024 * 1024
WHOLE = pl.BlockSpec(memory_space=pltpu.VMEM)
SCALARS = pl.BlockSpec(memory_space=pltpu.SMEM)
PARAMS = pltpu.CompilerParams(vmem_limit_bytes=VMEM_BYTES)


def iota(shape, dim):
    return lax.broadcasted_iota(jnp.int32, shape, dim)


def one_hot(shape, column_of_row):
    hit = iota(shape, 1) == column_of_row(iota(shape, 0))
    return jnp.where(hit, 1.0, 0.0).astype(BF16)


def dot(a, b):
    return jnp.dot(a, b, preferred_element_type=F32)


def split(a):
    high = a.astype(BF16)
    return high, (a - high.astype(F32)).astype(BF16)


def product(a, b):
    return dot(a[0], b[0]) + (dot(a[0], b[1]) + dot(a[1], b[0]))


def rounded(a):
    return a.astype(BF16).astype(F32)


def pick_kernel(chosen, ens, val, wgt, to_next, to_prev):
    row = iota((OWN, OBS), 0)
    for side, out in ((0, to_next), (1, to_prev)):
        for k in range(HANDED):
            block = chosen[side, k]
            at = pl.ds(pl.multiple_of(block * OBS, OBS), OBS)
            pert = ens[:, at].astype(F32)
            w = jnp.concatenate(
                [wgt[pl.ds(2 * block, 1), :], wgt[pl.ds(2 * block + 1, 1), :]], axis=1
            )
            v = jnp.concatenate(
                [val[pl.ds(2 * block, 1), :], val[pl.ds(2 * block + 1, 1), :]], axis=1
            )
            w_high, v_high = rounded(w), rounded(v)
            tail = jnp.where(
                row == 0,
                w_high,
                jnp.where(
                    row == 1,
                    w - w_high,
                    jnp.where(row == 2, v_high, jnp.where(row == 3, v - v_high, 0.0)),
                ),
            )
            out[:, k * OBS : (k + 1) * OBS] = jnp.concatenate([pert, tail], axis=0).astype(BF16)


def pack_kernel(fields, ens, left, right, out, wide):
    wide[:, LEVELS:, :] = jnp.zeros((OWN, 8 - LEVELS, wide.shape[2]), F32)
    wide[:, :LEVELS, :] = fields[...].astype(F32)
    order = one_hot((LEVELS * OWN, 64), lambda r: (r & 7) * 8 + (r >> 3))
    for peer in range(PEERS):
        rows = wide[:, :, peer * COLS : (peer + 1) * COLS].reshape(64, COLS).astype(BF16)
        out[peer, : LEVELS * OWN, :] = dot(order, rows).astype(BF16)
        if peer < 2:
            source, start = left, peer * 2 * OBS
        elif peer < PEERS - 2:
            source, start = ens, (peer - 2) * 2 * OBS
        else:
            source, start = right, (peer - PEERS + 2) * 2 * OBS
        first = source[:OWN, start : start + OBS].astype(F32)
        second = source[:OWN, start + OBS : start + 2 * OBS].astype(F32)
        out[peer, LEVELS * OWN :, :] = jnp.concatenate([first, second], axis=0).astype(BF16)


def gram_kernel(me, table, damping, tally, pert, val, wgt, left, right, out):
    wide = pert[...].astype(F32)
    lane = iota((128, 128), 1)
    row = iota((128, 128), 0) & 3
    block_of_lane = iota((1, 128), 1) - 64
    top, low = [], []
    for half in range(2):
        block = 2 * me[0] + half
        own = jnp.clip(block - HANDED, 0, HOME - 1)
        w = jnp.concatenate(
            [wgt[pl.ds(2 * own, 1), :], wgt[pl.ds(2 * own + 1, 1), :]], axis=1
        )
        v = jnp.concatenate(
            [val[pl.ds(2 * own, 1), :], val[pl.ds(2 * own + 1, 1), :]], axis=1
        )
        from_left = jnp.clip(block, 0, HANDED - 1)
        from_right = jnp.clip(block - HANDED - HOME, 0, HANDED - 1)
        at_left = left[:, pl.ds(pl.multiple_of(from_left * OBS, OBS), OBS)].astype(F32)
        at_right = right[:, pl.ds(pl.multiple_of(from_right * OBS, OBS), OBS)].astype(F32)
        is_left = block < HANDED
        is_right = block >= HANDED + HOME
        w = jnp.where(
            is_left,
            at_left[8:9] + at_left[9:10],
            jnp.where(is_right, at_right[8:9] + at_right[9:10], w),
        )
        v = jnp.where(
            is_left,
            at_left[10:11] + at_left[11:12],
            jnp.where(is_right, at_right[10:11] + at_right[11:12], v),
        )
        y = wide[:, half * OWN : (half + 1) * OWN, :].reshape(MEMBERS, OBS)
        scaled = (y * w).astype(BF16)
        gram = lax.dot_general(
            y.astype(BF16), scaled, (((1,), (1,)), ((), ())), preferred_element_type=F32
        )
        vector = jnp.sum(y * (w * v), axis=1, keepdims=True)
        vector_high = rounded(vector)
        vector_low = vector - vector_high
        coeff = jnp.zeros((1, 128), F32)
        for position in range(MAXL):
            used = jnp.where(position < tally[half], damping[half, position], 0.0)
            coeff = coeff + jnp.where(block_of_lane == table[half, position], used, 0.0)
        coeff_high = rounded(coeff)
        extra = jnp.where(row == 0, coeff_high, jnp.where(row == 1, coeff - coeff_high, 0.0))
        for place, column in enumerate(
            (vector_high[:128], vector_low[:128], vector_high[128:], vector_low[128:])
        ):
            extra = jnp.where(lane == place, column, extra)
        top.append(gram[:128, :])
        low.append(jnp.concatenate([gram[128:, 128:], extra], axis=1))
    stacked = jnp.concatenate(top + low, axis=0).astype(BF16)
    order = one_hot(
        (512, 512), lambda r: ((r >> 3) & 1) * 256 + ((r >> 2) & 1) * 128 + (r >> 4) * 4 + (r & 3)
    )
    out[...] = dot(order, stacked).reshape(PEERS, 16, 256).astype(BF16)


def combine_kernel(entries, out):
    x = entries[...].astype(F32).reshape(512, 256).astype(BF16)
    coeffs = x[:, 128:]
    row = iota((512, 512), 0)
    column = iota((512, 512), 1)
    same = ((row ^ column) & 11) == 0
    spread_out = jnp.where(
        iota((128, 512), 0) - 64
        == 2 * (iota((128, 512), 1) >> 4) + ((iota((128, 512), 1) >> 2) & 1),
        1.0,
        0.0,
    ).astype(BF16)
    total = None
    for part in range(2):
        take = one_hot((512, 512), lambda r: (r & ~15) + 8 + (r & 4) + part)
        wide = dot(dot(take, coeffs).astype(BF16), spread_out)
        term = dot(jnp.where(same, wide, 0.0).astype(BF16), x)
        total = term if total is None else total + term
    tail = total[:, 128:]
    both = tail + pltpu.roll(tail, 127, 1)
    high = rounded(both)
    low = pltpu.roll(both - high, 1, 1)
    lane = iota((512, 128), 1)
    has_vector = ((iota((512, 128), 0) & 8) != 0) & (lane < 4)
    tail = jnp.where(has_vector, jnp.where((lane & 1) == 0, high, low), tail)
    out[...] = (
        jnp.concatenate([total[:, :128], tail], axis=1).reshape(PEERS, 16, 256).astype(BF16)
    )


def centre_kernel(fields, pert, centre):
    wide = fields[...].astype(F32)
    for level in range(LEVELS):
        x = wide[:, level * OWN : (level + 1) * OWN, :].reshape(MEMBERS, COLS)
        mean = jnp.sum(x, axis=0, keepdims=True) / MEMBERS
        away = (x - mean).astype(BF16)
        for half in range(2):
            at = slice(level * 128, (level + 1) * 128)
            pert[half, :, at] = away[:, half * 128 : (half + 1) * 128]
            centre[half, :, at] = jnp.broadcast_to(
                mean[:, half * 128 : (half + 1) * 128], (8, 128)
            )


def mix_kernel(entries, pert, centre, out):
    x = entries[...].astype(F32).reshape(512, 256).astype(BF16)
    order = one_hot(
        (512, 512), lambda r: ((r & 127) >> 2) * 16 + (r >> 8) * 8 + ((r >> 7) & 1) * 4 + (r & 3)
    )
    sorted_rows = dot(order, x)
    eye = jnp.where(iota((256, 256), 0) == iota((256, 256), 1), 1.0, 0.0)
    vectors, bounds, a1 = [], [], []
    for half in range(2):
        top = sorted_rows[half * 128 : (half + 1) * 128]
        low = sorted_rows[256 + half * 128 : 256 + (half + 1) * 128]
        gram = jnp.concatenate(
            [top, jnp.concatenate([top[:, 128:].T, low[:, :128]], axis=1)], axis=0
        )
        vectors.append(
            jnp.concatenate(
                [low[:, 128:129] + low[:, 129:130], low[:, 130:131] + low[:, 131:132]], axis=0
            )
        )
        system = eye + gram * (1.0 / (MEMBERS - 1.0))
        sums = jnp.sum(jnp.abs(system), axis=1, keepdims=True)
        bound = jnp.max(sums, axis=0, keepdims=True)
        bounds.append(bound)
        a1.append(system / bound)
    s1 = [split(a) for a in a1]
    a2 = [product(s, s) for s in s1]
    s2 = [split(a) for a in a2]
    a3 = [product(s, t) for s, t in zip(s2, s1)]
    a4 = [product(s, s) for s in s2]
    z2 = [
        2.25 * eye - 2.4375 * a + 1.6875 * b - 0.5625 * c + 0.0625 * d
        for a, b, c, d in zip(a1, a2, a3, a4)
    ]
    t2 = [split(z) for z in z2]
    az = [split(product(s, t)) for s, t in zip(s1, t2)]
    zz = [split(product(t, t)) for t in t2]
    z3 = [1.5 * z - 0.5 * product(a, b) for z, a, b in zip(z2, az, zz)]
    for half in range(2):
        spread = z3[half] / jnp.sqrt(bounds[half])
        inner = jnp.sum(spread * vectors[half], axis=0, keepdims=True)
        shift = jnp.sum(spread * inner, axis=1, keepdims=True) / (MEMBERS - 1.0)
        mixing = (spread + shift).T.astype(BF16)
        result = dot(mixing, pert[half]) + centre[half][:1]
        for pair in range(LEVELS // 2):
            rows = jnp.concatenate(
                [
                    result[:, level * 128 : (level + 1) * 128].reshape(PEERS, OWN, 128)
                    for level in (2 * pair, 2 * pair + 1)
                ],
                axis=1,
            )
            out[:, pair * 16 : (pair + 1) * 16, half * 128 : (half + 1) * 128] = rows.astype(BF16)


def unpack_kernel(parts, out):
    order = one_hot((64, LEVELS * OWN), lambda r: (r & 7) * 8 + (r >> 3))
    for peer in range(PEERS):
        rows = dot(order, parts[peer]).reshape(OWN, 8, COLS)
        out[:, :, peer * COLS : (peer + 1) * COLS] = rows[:, :LEVELS].astype(BF16)


def shifted(value, by):
    length = lax.axis_size("region")
    pairs = [(i, i + by) for i in range(length) if 0 <= i + by < length]
    return lax.ppermute(value, "region", pairs)


def exchange(value):
    return lax.all_to_all(value, "member", split_axis=0, concat_axis=0, tiled=True)


def shape(*dims, dtype=BF16):
    return jax.ShapeDtypeStruct(dims, dtype)


def on_device(
    background_trajectories,
    sensor_spread_matrix,
    departure_vector,
    inverse_error_variance,
    edge_tile_handoff,
    measurement_tile_table,
    distance_damping,
    active_tile_tally,
):
    val = departure_vector.reshape(2 * HOME, 128)
    wgt = inverse_error_variance.reshape(2 * HOME, 128)
    me = lax.axis_index("member").reshape(1)

    to_next, to_prev = pl.pallas_call(
        pick_kernel,
        out_shape=(shape(16, HANDED * OBS), shape(16, HANDED * OBS)),
        in_specs=[SCALARS, WHOLE, WHOLE, WHOLE],
        out_specs=(WHOLE, WHOLE),
        compiler_params=PARAMS,
        name="pick",
    )(edge_tile_handoff, sensor_spread_matrix, val, wgt)
    left = shifted(to_next, 1)
    right = shifted(to_prev, -1)

    packed = pl.pallas_call(
        pack_kernel,
        out_shape=shape(PEERS, 64, COLS),
        in_specs=[WHOLE] * 4,
        out_specs=WHOLE,
        scratch_shapes=[pltpu.VMEM((OWN, 8, PEERS * COLS), F32)],
        compiler_params=PARAMS,
        name="pack",
    )(background_trajectories, sensor_spread_matrix, left, right)
    gathered = exchange(packed)

    grams = pl.pallas_call(
        gram_kernel,
        grid=(1,),
        out_shape=shape(PEERS, 16, 256),
        in_specs=[SCALARS] * 4
        + [pl.BlockSpec((PEERS, 16, COLS), lambda i: (0, 3, 0))]
        + [WHOLE] * 4,
        out_specs=pl.BlockSpec((PEERS, 16, 256), lambda i: (0, 0, 0)),
        compiler_params=PARAMS,
        name="gram",
    )(
        me,
        measurement_tile_table,
        distance_damping,
        active_tile_tally,
        gathered,
        val,
        wgt,
        left,
        right,
    )
    entries = exchange(grams)

    pert, centre = pl.pallas_call(
        centre_kernel,
        grid=(1,),
        out_shape=(shape(2, MEMBERS, LEVELS * 128), shape(2, 8, LEVELS * 128, dtype=F32)),
        in_specs=[pl.BlockSpec((PEERS, LEVELS * OWN, COLS), lambda i: (0, 0, 0))],
        out_specs=(
            pl.BlockSpec((2, MEMBERS, LEVELS * 128), lambda i: (0, 0, 0)),
            pl.BlockSpec((2, 8, LEVELS * 128), lambda i: (0, 0, 0)),
        ),
        compiler_params=PARAMS,
        name="centre",
    )(gathered)

    sums = pl.pallas_call(
        combine_kernel,
        out_shape=shape(PEERS, 16, 256),
        in_specs=[WHOLE],
        out_specs=WHOLE,
        compiler_params=PARAMS,
        name="combine",
    )(entries)
    systems = exchange(sums)

    mixed = pl.pallas_call(
        mix_kernel,
        out_shape=shape(PEERS, LEVELS * OWN, COLS),
        in_specs=[WHOLE] * 3,
        out_specs=WHOLE,
        compiler_params=PARAMS,
        name="mix",
    )(systems, pert, centre)
    returned = exchange(mixed)

    return pl.pallas_call(
        unpack_kernel,
        out_shape=shape(OWN, LEVELS, PEERS * COLS),
        in_specs=[WHOLE],
        out_specs=WHOLE,
        compiler_params=PARAMS,
        name="unpack",
    )(returned)


def solution(mesh):
    placed = (
        P("member", None, "region"),
        P("member", "region"),
        P("region"),
        P("region"),
        P(None, "region"),
        P(("region", "member"), None),
        P(("region", "member"), None),
        P(("region", "member")),
    )
    return jax.shard_map(
        on_device,
        mesh=mesh,
        in_specs=placed,
        out_specs=P("member", None, "region"),
        check_vma=False,
    )
```

```python
import jax
import jax.numpy as jnp
from jax import lax
from jax.experimental import pallas as pl
from jax.experimental.pallas import tpu as pltpu
from jax.sharding import PartitionSpec as P

F32 = jnp.float32
BF16 = jnp.bfloat16
MEMBERS = 256
PEERS = 32
OWN = 8
LEVELS = 6
OBS = 256
HANDED = 4
HOME = 56
EXT = 64
COLS = 256
MAXL = 16
VMEM_BYTES = 48 * 1024 * 1024
WHOLE = pl.BlockSpec(memory_space=pltpu.VMEM)
ANY = pl.BlockSpec(memory_space=pl.ANY)
HBM = pl.BlockSpec(memory_space=pltpu.HBM)
SCALARS = pl.BlockSpec(memory_space=pltpu.SMEM)
SPLIT = True
PARAMS = pltpu.CompilerParams(vmem_limit_bytes=VMEM_BYTES)


def iota(shape, dim):
    return lax.broadcasted_iota(jnp.int32, shape, dim)


def one_hot(shape, column_of_row):
    hit = iota(shape, 1) == column_of_row(iota(shape, 0))
    return jnp.where(hit, 1.0, 0.0).astype(BF16)


def dot(a, b):
    return jnp.dot(a, b, preferred_element_type=F32)


def split(a):
    high = a.astype(BF16)
    return high, (a - high.astype(F32)).astype(BF16)


def product(a, b):
    return dot(a[0], b[0]) + (dot(a[0], b[1]) + dot(a[1], b[0]))


def rounded(a):
    return a.astype(BF16).astype(F32)


def in_flight(pairs, sems):
    copies = [pltpu.make_async_copy(*ends, sems.at[k]) for k, ends in enumerate(pairs)]
    for copy in copies:
        copy.start()
    return copies


def landed(copies):
    for copy in copies:
        copy.wait()


def wide_row(pair):
    return jnp.concatenate([pair[:1], pair[1:]], axis=1)


def pick_kernel(chosen, blocks, val, wgt, to_next, to_prev, vals, wgts, sems):
    pairs = []
    for side, out in ((0, to_next), (1, to_prev)):
        for k in range(HANDED):
            block = chosen[side, k]
            pairs += [
                (blocks.at[block], out.at[k]),
                (val.at[block], vals.at[side * HANDED + k]),
                (wgt.at[block], wgts.at[side * HANDED + k]),
            ]
    landed(in_flight(pairs, sems))
    row = iota((OWN, OBS), 0)
    for side, out in ((0, to_next), (1, to_prev)):
        for k in range(HANDED):
            w = wide_row(wgts[side * HANDED + k])
            v = wide_row(vals[side * HANDED + k])
            w_high, v_high = rounded(w), rounded(v)
            tail = jnp.where(row == 2, v_high, jnp.where(row == 3, v - v_high, 0.0))
            tail = jnp.where(row == 0, w_high, jnp.where(row == 1, w - w_high, tail))
            out[HANDED + k] = tail.astype(BF16)


def own_pairs(blocks, left, right, out, group):
    pairs = []
    for peer in range(PEERS):
        if peer < 2:
            source = left.at[pl.ds(2 * peer, 2)]
        elif peer < PEERS - 2:
            source = blocks.at[pl.ds(2 * peer - HANDED, 2)]
        else:
            source = right.at[pl.ds(2 * (peer - PEERS + 2), 2)]
        pairs.append((source, out.at[peer, pl.ds(group, 2)]))
    return pairs


def field_pairs(fields, out):
    return [
        (fields.at[:, :, pl.ds(peer * COLS, COLS)], out.at[peer, pl.ds(0, LEVELS)])
        for peer in range(PEERS)
    ]


def pack_both_kernel(fields, blocks, left, right, out, sems):
    pairs = field_pairs(fields, out) + own_pairs(blocks, left, right, out, LEVELS)
    landed(in_flight(pairs, sems))


def pack_blocks_kernel(blocks, left, right, out, sems):
    landed(in_flight(own_pairs(blocks, left, right, out, 0), sems))


def grams_of(me, table, damping, tally, val, wgt, left, right, pert):
    lane = iota((128, 128), 1)
    row = iota((128, 128), 0) & 3
    block_of_lane = iota((1, 128), 1) - 64
    top, low = [], []
    for half in range(2):
        block = 2 * me[0] + half
        own = jnp.clip(block - HANDED, 0, HOME - 1)
        w, v = wide_row(wgt[own]), wide_row(val[own])
        at_left = left[HANDED + jnp.clip(block, 0, HANDED - 1)].astype(F32)
        at_right = right[HANDED + jnp.clip(block - HANDED - HOME, 0, HANDED - 1)].astype(F32)
        is_left = block < HANDED
        is_right = block >= HANDED + HOME
        w = jnp.where(
            is_left,
            at_left[0:1] + at_left[1:2],
            jnp.where(is_right, at_right[0:1] + at_right[1:2], w),
        )
        v = jnp.where(
            is_left,
            at_left[2:3] + at_left[3:4],
            jnp.where(is_right, at_right[2:3] + at_right[3:4], v),
        )
        y = pert(half).astype(F32).reshape(MEMBERS, OBS)
        scaled = (y * w).astype(BF16)
        gram = lax.dot_general(
            y.astype(BF16), scaled, (((1,), (1,)), ((), ())), preferred_element_type=F32
        )
        vector = jnp.sum(y * (w * v), axis=1, keepdims=True)
        vector_high = rounded(vector)
        vector_low = vector - vector_high
        coeff = jnp.zeros((1, 128), F32)
        for position in range(MAXL):
            used = jnp.where(position < tally[half], damping[half, position], 0.0)
            coeff = coeff + jnp.where(block_of_lane == table[half, position], used, 0.0)
        coeff_high = rounded(coeff)
        extra = jnp.where(row == 0, coeff_high, jnp.where(row == 1, coeff - coeff_high, 0.0))
        for place, column in enumerate(
            (vector_high[:128], vector_low[:128], vector_high[128:], vector_low[128:])
        ):
            extra = jnp.where(lane == place, column, extra)
        top.append(gram[:128, :])
        low.append(jnp.concatenate([gram[128:, 128:], extra], axis=1))
    stacked = jnp.concatenate(top + low, axis=0).astype(BF16)
    order = one_hot(
        (512, 512), lambda r: ((r >> 3) & 1) * 256 + ((r >> 2) & 1) * 128 + (r >> 4) * 4 + (r & 3)
    )
    return dot(order, stacked).reshape(PEERS, 2, 8, 256).astype(BF16)


def gram_kernel(me, table, damping, tally, val, wgt, left, right, gathered, out):
    group = gathered.shape[1] - 2
    out[...] = grams_of(
        me, table, damping, tally, val, wgt, left, right, lambda half: gathered[:, group + half]
    )


def gram_and_pack_kernel(
    me, table, damping, tally, val, wgt, left, right, gathered, fields, out, grams, sems
):
    copies = in_flight(field_pairs(fields, out), sems)
    grams[...] = grams_of(
        me, table, damping, tally, val, wgt, left, right, lambda half: gathered[:, half]
    )
    last = pltpu.make_async_copy(grams, out.at[:, pl.ds(LEVELS, 2)], sems.at[PEERS])
    last.start()
    landed(copies)
    last.wait()


def combine_kernel(entries, out):
    group = entries.shape[1] - 2
    x = entries[:, group:].astype(F32).reshape(512, 256).astype(BF16)
    coeffs = x[:, 128:]
    row = iota((512, 512), 0)
    column = iota((512, 512), 1)
    same = ((row ^ column) & 11) == 0
    spread_out = jnp.where(
        iota((128, 512), 0) - 64
        == 2 * (iota((128, 512), 1) >> 4) + ((iota((128, 512), 1) >> 2) & 1),
        1.0,
        0.0,
    ).astype(BF16)
    total = None
    for part in range(2):
        take = one_hot((512, 512), lambda r: (r & ~15) + 8 + (r & 4) + part)
        wide = dot(dot(take, coeffs).astype(BF16), spread_out)
        term = dot(jnp.where(same, wide, 0.0).astype(BF16), x)
        total = term if total is None else total + term
    tail = total[:, 128:]
    both = tail + pltpu.roll(tail, 127, 1)
    high = rounded(both)
    low = pltpu.roll(both - high, 1, 1)
    lane = iota((512, 128), 1)
    has_vector = ((iota((512, 128), 0) & 8) != 0) & (lane < 4)
    tail = jnp.where(has_vector, jnp.where((lane & 1) == 0, high, low), tail)
    out[...] = (
        jnp.concatenate([total[:, :128], tail], axis=1).reshape(PEERS, 2, 8, 256).astype(BF16)
    )


def centre_kernel(fields, pert, centre):
    for level in range(LEVELS):
        x = fields[:, level].astype(F32).reshape(MEMBERS, COLS)
        mean = jnp.sum(x, axis=0, keepdims=True) / MEMBERS
        away = (x - mean).astype(BF16)
        for half in range(2):
            at = slice(level * 128, (level + 1) * 128)
            pert[half, :, at] = away[:, half * 128 : (half + 1) * 128]
            centre[half, :, at] = jnp.broadcast_to(
                mean[:, half * 128 : (half + 1) * 128], (8, 128)
            )


def mix_kernel(entries, pert, centre, out):
    x = entries[...].astype(F32).reshape(512, 256).astype(BF16)
    order = one_hot(
        (512, 512), lambda r: ((r & 127) >> 2) * 16 + (r >> 8) * 8 + ((r >> 7) & 1) * 4 + (r & 3)
    )
    sorted_rows = dot(order, x)
    eye = jnp.where(iota((256, 256), 0) == iota((256, 256), 1), 1.0, 0.0)
    vectors, bounds, a1 = [], [], []
    for half in range(2):
        top = sorted_rows[half * 128 : (half + 1) * 128]
        low = sorted_rows[256 + half * 128 : 256 + (half + 1) * 128]
        gram = jnp.concatenate(
            [top, jnp.concatenate([top[:, 128:].T, low[:, :128]], axis=1)], axis=0
        )
        vectors.append(
            jnp.concatenate(
                [low[:, 128:129] + low[:, 129:130], low[:, 130:131] + low[:, 131:132]], axis=0
            )
        )
        system = eye + gram * (1.0 / (MEMBERS - 1.0))
        sums = jnp.sum(jnp.abs(system), axis=1, keepdims=True)
        bound = jnp.max(sums, axis=0, keepdims=True)
        bounds.append(bound)
        a1.append(system / bound)
    s1 = [split(a) for a in a1]
    a2 = [product(s, s) for s in s1]
    s2 = [split(a) for a in a2]
    a3 = [product(s, t) for s, t in zip(s2, s1)]
    a4 = [product(s, s) for s in s2]
    z2 = [
        2.25 * eye - 2.4375 * a + 1.6875 * b - 0.5625 * c + 0.0625 * d
        for a, b, c, d in zip(a1, a2, a3, a4)
    ]
    t2 = [split(z) for z in z2]
    az = [split(product(s, t)) for s, t in zip(s1, t2)]
    zz = [split(product(t, t)) for t in t2]
    z3 = [1.5 * z - 0.5 * product(a, b) for z, a, b in zip(z2, az, zz)]
    for half in range(2):
        spread = z3[half] / jnp.sqrt(bounds[half])
        inner = jnp.sum(spread * vectors[half], axis=0, keepdims=True)
        shift = jnp.sum(spread * inner, axis=1, keepdims=True) / (MEMBERS - 1.0)
        mixing = (spread + shift).T.astype(BF16)
        result = dot(mixing, pert[half]) + centre[half][:1]
        for level in range(LEVELS):
            rows = result[:, level * 128 : (level + 1) * 128].reshape(PEERS, OWN, 128)
            out[:, level, :, half * 128 : (half + 1) * 128] = rows.astype(BF16)


def unpack_kernel(parts, out, sems):
    copies = [
        pltpu.make_async_copy(
            parts.at[peer], out.at[:, :, pl.ds(peer * COLS, COLS)], sems.at[peer]
        )
        for peer in range(PEERS)
    ]
    for copy in copies:
        copy.start()
    for copy in copies:
        copy.wait()


def shifted(value, by):
    length = lax.axis_size("region")
    pairs = [(i, i + by) for i in range(length) if 0 <= i + by < length]
    return lax.ppermute(value, "region", pairs)


def exchange(value):
    return lax.all_to_all(value, "member", split_axis=0, concat_axis=0, tiled=True)


def shape(*dims, dtype=BF16):
    return jax.ShapeDtypeStruct(dims, dtype)


def on_device(
    background_trajectories,
    sensor_spread_matrix,
    departure_vector,
    inverse_error_variance,
    edge_tile_handoff,
    measurement_tile_table,
    distance_damping,
    active_tile_tally,
):
    val = departure_vector.reshape(HOME, 2, 128)
    wgt = inverse_error_variance.reshape(HOME, 2, 128)
    fields = background_trajectories.transpose(1, 0, 2)
    blocks = sensor_spread_matrix.reshape(OWN, HOME, OBS).transpose(1, 0, 2)
    me = lax.axis_index("member").reshape(1)

    to_next, to_prev = pl.pallas_call(
        pick_kernel,
        out_shape=(shape(2 * HANDED, OWN, OBS),) * 2,
        in_specs=[SCALARS, HBM, HBM, HBM],
        out_specs=(WHOLE, WHOLE),
        scratch_shapes=[
            pltpu.VMEM((2 * HANDED, 2, 128), F32),
            pltpu.VMEM((2 * HANDED, 2, 128), F32),
            pltpu.SemaphoreType.DMA((6 * HANDED,)),
        ],
        compiler_params=PARAMS,
        name="pick",
    )(edge_tile_handoff, blocks, val, wgt)
    left = shifted(to_next, 1)
    right = shifted(to_prev, -1)

    about = (me, measurement_tile_table, distance_damping, active_tile_tally, val, wgt)

    def fields_first(fields, blocks, left, right, *about):
        packed = pl.pallas_call(
            pack_both_kernel,
            out_shape=shape(PEERS, LEVELS + 2, OWN, COLS),
            in_specs=[HBM, HBM, ANY, ANY],
            out_specs=ANY,
            scratch_shapes=[pltpu.SemaphoreType.DMA((2 * PEERS,))],
            compiler_params=PARAMS,
            name="pack_both",
        )(fields, blocks, left, right)
        gathered = exchange(packed)
        grams = pl.pallas_call(
            gram_kernel,
            out_shape=shape(PEERS, 2, 8, 256),
            in_specs=[SCALARS] * 4 + [WHOLE] * 5,
            out_specs=WHOLE,
            compiler_params=PARAMS,
            name="gram",
        )(*about, left, right, gathered)
        return finish(exchange(grams), gathered)

    def fields_second(fields, blocks, left, right, *about):
        packed = pl.pallas_call(
            pack_blocks_kernel,
            out_shape=shape(PEERS, 2, OWN, COLS),
            in_specs=[HBM, ANY, ANY],
            out_specs=ANY,
            scratch_shapes=[pltpu.SemaphoreType.DMA((PEERS,))],
            compiler_params=PARAMS,
            name="pack_blocks",
        )(blocks, left, right)
        gathered = exchange(packed)
        grams = pl.pallas_call(
            gram_and_pack_kernel,
            out_shape=shape(PEERS, LEVELS + 2, OWN, COLS),
            in_specs=[SCALARS] * 4 + [WHOLE] * 5 + [HBM],
            out_specs=ANY,
            scratch_shapes=[
                pltpu.VMEM((PEERS, 2, 8, 256), BF16),
                pltpu.SemaphoreType.DMA((PEERS + 1,)),
            ],
            compiler_params=PARAMS,
            name="gram_and_pack",
        )(*about, left, right, gathered, fields)
        entries = exchange(grams)
        return finish(entries, entries)

    operands = (fields, blocks, left, right, *about)
    if SPLIT:
        even = lax.axis_index("region") % 2 == 0
        analysis = lax.cond(even, fields_first, fields_second, *operands)
    else:
        analysis = fields_first(*operands)
    return analysis.transpose(1, 0, 2)


def finish(entries, gathered):
    pert, centre = pl.pallas_call(
        centre_kernel,
        out_shape=(shape(2, MEMBERS, LEVELS * 128), shape(2, 8, LEVELS * 128, dtype=F32)),
        in_specs=[WHOLE],
        out_specs=(WHOLE, WHOLE),
        compiler_params=PARAMS,
        name="centre",
    )(gathered)
    sums = pl.pallas_call(
        combine_kernel,
        out_shape=shape(PEERS, 2, 8, 256),
        in_specs=[WHOLE],
        out_specs=WHOLE,
        compiler_params=PARAMS,
        name="combine",
    )(entries)
    mixed = pl.pallas_call(
        mix_kernel,
        out_shape=shape(PEERS, LEVELS, OWN, COLS),
        in_specs=[WHOLE] * 3,
        out_specs=WHOLE,
        compiler_params=PARAMS,
        name="mix",
    )(exchange(sums), pert, centre)
    return pl.pallas_call(
        unpack_kernel,
        out_shape=shape(LEVELS, OWN, PEERS * COLS),
        in_specs=[ANY],
        out_specs=HBM,
        scratch_shapes=[pltpu.SemaphoreType.DMA((PEERS,))],
        compiler_params=PARAMS,
        name="unpack",
    )(exchange(mixed))


def solution(mesh):
    placed = (
        P("member", None, "region"),
        P("member", "region"),
        P("region"),
        P("region"),
        P(None, "region"),
        P(("region", "member"), None),
        P(("region", "member"), None),
        P(("region", "member")),
    )
    return jax.shard_map(
        on_device,
        mesh=mesh,
        in_specs=placed,
        out_specs=P("member", None, "region"),
        check_vma=False,
    )
```

```python
import jax
import jax.numpy as jnp
from jax import lax
from jax.experimental import pallas as pl
from jax.experimental.pallas import tpu as pltpu
from jax.sharding import PartitionSpec as P

F32 = jnp.float32
BF16 = jnp.bfloat16
MEMBERS = 256
PEERS = 32
OWN = 8
LEVELS = 6
OBS = 256
HANDED = 4
HOME = 56
EXT = 64
COLS = 256
MAXL = 16
VMEM_BYTES = 48 * 1024 * 1024
WHOLE = pl.BlockSpec(memory_space=pltpu.VMEM)
ANY = pl.BlockSpec(memory_space=pl.ANY)
HBM = pl.BlockSpec(memory_space=pltpu.HBM)
SCALARS = pl.BlockSpec(memory_space=pltpu.SMEM)
PARAMS = pltpu.CompilerParams(vmem_limit_bytes=VMEM_BYTES)


def iota(shape, dim):
    return lax.broadcasted_iota(jnp.int32, shape, dim)


def one_hot_lanes(shape):
    hit = iota(shape, 0) - 64 == (iota(shape, 1) >> 2)
    return jnp.where(hit, 1.0, 0.0).astype(BF16)


def dot(a, b):
    return jnp.dot(a, b, preferred_element_type=F32)


def split(a):
    high = a.astype(BF16)
    return high, (a - high.astype(F32)).astype(BF16)


def product(a, b):
    return dot(a[0], b[0]) + (dot(a[0], b[1]) + dot(a[1], b[0]))


def rounded(a):
    return a.astype(BF16).astype(F32)


def in_flight(pairs, sems):
    copies = [pltpu.make_async_copy(*ends, sems.at[k]) for k, ends in enumerate(pairs)]
    for copy in copies:
        copy.start()
    return copies


def landed(copies):
    for copy in copies:
        copy.wait()


def wide_row(pair):
    return jnp.concatenate([pair[:1], pair[1:]], axis=1)


def own_pairs(blocks, zeros, out, group):
    zeros[...] = jnp.zeros(zeros.shape, BF16)
    return [
        (
            blocks.at[pl.ds(2 * peer, 2)] if 2 * peer < HOME else zeros,
            out.at[peer, pl.ds(group, 2)],
        )
        for peer in range(PEERS)
    ]


def field_pairs(fields, out):
    return [
        (fields.at[:, :, pl.ds(peer * COLS, COLS)], out.at[peer, pl.ds(0, LEVELS)])
        for peer in range(PEERS)
    ]


def pack_both_kernel(fields, blocks, out, zeros, sems):
    pairs = field_pairs(fields, out) + own_pairs(blocks, zeros, out, LEVELS)
    landed(in_flight(pairs, sems))


def pack_blocks_kernel(blocks, out, zeros, sems):
    landed(in_flight(own_pairs(blocks, zeros, out, 0), sems))


def first_half(rows):
    return iota(rows.shape, 1) < 4


def interleaved(first, second):
    first, second = (rows.reshape(16, 8, 256) for rows in (first, second))
    here = first_half(first)
    even = jnp.where(here, first, pltpu.roll(second, 4, 1))
    odd = jnp.where(here, pltpu.roll(first, 4, 1), second)
    return jnp.stack([even, odd], axis=1).reshape(PEERS, 8, 256)


def separated(rows):
    rows = rows.reshape(16, 2, 8, 256)
    even, odd = rows[:, 0], rows[:, 1]
    here = first_half(even)
    first = jnp.where(here, even, pltpu.roll(odd, 4, 1))
    second = jnp.where(here, pltpu.roll(even, 4, 1), odd)
    return first.reshape(128, 256), second.reshape(128, 256)


def grams_of(me, table, damping, tally, val, wgt, pert):
    lane = iota((128, 128), 1)
    row = iota((128, 128), 0) & 3
    slot_of_lane = iota((1, 128), 1) - 64
    top, low = [], []
    for half in range(2):
        own = jnp.minimum(2 * me[0] + half, HOME - 1)
        w, v = wide_row(wgt[own]), wide_row(val[own])
        y = pert(half).astype(F32).reshape(MEMBERS, OBS)
        scaled = (y * w).astype(BF16)
        gram = lax.dot_general(
            y.astype(BF16), scaled, (((1,), (1,)), ((), ())), preferred_element_type=F32
        )
        vector = jnp.sum(y * (w * v), axis=1, keepdims=True)
        vector_high = rounded(vector)
        vector_low = vector - vector_high
        coeff = jnp.zeros((1, 128), F32)
        for position in range(MAXL):
            used = jnp.where(position < tally[half], damping[half, position], 0.0)
            slot = (table[half, position] - HANDED) & (EXT - 1)
            coeff = coeff + jnp.where(slot_of_lane == slot, used, 0.0)
        coeff_high = rounded(coeff)
        extra = jnp.where(row == 0, coeff_high, jnp.where(row == 1, coeff - coeff_high, 0.0))
        for place, column in enumerate(
            (vector_high[:128], vector_low[:128], vector_high[128:], vector_low[128:])
        ):
            extra = jnp.where(lane == place, column, extra)
        top.append(gram[:128, :])
        low.append(jnp.concatenate([gram[128:, 128:], extra], axis=1))
    return interleaved(*top).astype(BF16), interleaved(*low).astype(BF16)


def gram_kernel(me, table, damping, tally, val, wgt, gathered, out):
    out[:, 0], out[:, 1] = grams_of(
        me, table, damping, tally, val, wgt, lambda half: gathered[:, LEVELS + half]
    )


def gram_and_pack_kernel(
    me, table, damping, tally, val, wgt, gathered, fields, out, grams, sems
):
    copies = in_flight(field_pairs(fields, out), sems)
    grams[:, 0], grams[:, 1] = grams_of(
        me, table, damping, tally, val, wgt, lambda half: gathered[:, half]
    )
    last = pltpu.make_async_copy(grams, out.at[:, pl.ds(LEVELS, 2)], sems.at[PEERS])
    last.start()
    landed(copies)
    last.wait()


def choose_kernel(region, chosen, entries, across, within):
    odd = region[0] & 1
    here = iota((2, 8, 256), 1) < 4
    for side, out in ((1 - odd, across), (odd, within)):
        for pair in range(HANDED // 2):
            rows = []
            for k in range(2):
                block = chosen[side, 2 * pair + k]
                x = entries[block >> 1].astype(F32)
                rows.append(jnp.where((block & 1) == k, x, pltpu.roll(x, 4, 1)))
            out[pair] = jnp.where(here, rows[0], rows[1]).astype(BF16)


def combine_kernel(region, entries, across, within, out):
    x = entries[...].astype(F32)
    coeffs = x[:, 1, :, 128:]
    here = first_half(coeffs)
    high = jnp.where(here, coeffs[:, 0:1], coeffs[:, 4:5]).reshape(256, 128)
    low = jnp.where(here, coeffs[:, 1:2], coeffs[:, 5:6]).reshape(256, 128)
    spread_out = one_hot_lanes((128, 256))
    wide = dot(jnp.concatenate([high, low], axis=0).astype(BF16), spread_out)
    same = ((iota((256, 256), 0) ^ iota((256, 256), 1)) & 3) == 0
    high = jnp.where(same, wide[:256], 0.0).astype(BF16)
    low = jnp.where(same, wide[256:], 0.0).astype(BF16)

    odd = (region[0] & 1) == 1
    across, within = across[...].astype(F32), within[...].astype(F32)
    left = jnp.where(odd, within, across)
    right = jnp.where(odd, across, within)
    total = []
    for part in range(2):
        handed = jnp.concatenate([right[:, part], left[:, part]], axis=0)
        if part == 1:
            keep = iota(handed.shape, 2) >= 192
            handed = jnp.where(keep, x[HOME // 2 :, part], handed)
        rows = jnp.concatenate([x[: HOME // 2, part], handed], axis=0)
        rows = rows.reshape(256, 256).astype(BF16)
        total.append(dot(high, rows) + dot(low, rows))
    tail = total[1][:, 128:]
    both = tail + pltpu.roll(tail, 127, 1)
    high = rounded(both)
    low = pltpu.roll(both - high, 1, 1)
    lane = iota((256, 128), 1)
    tail = jnp.where(lane < 4, jnp.where((lane & 1) == 0, high, low), tail)
    tail = jnp.concatenate([total[1][:, :128], tail], axis=1)
    out[:, 0] = total[0].reshape(PEERS, 8, 256).astype(BF16)
    out[:, 1] = tail.reshape(PEERS, 8, 256).astype(BF16)


def centre_kernel(fields, pert, centre, entries=None):
    if entries is not None:
        entries[...] = fields[:, LEVELS:]
    for level in range(LEVELS):
        x = fields[:, level].astype(F32).reshape(MEMBERS, COLS)
        mean = jnp.sum(x, axis=0, keepdims=True) / MEMBERS
        away = (x - mean).astype(BF16)
        for half in range(2):
            at = slice(level * 128, (level + 1) * 128)
            pert[half, :, at] = away[:, half * 128 : (half + 1) * 128]
            centre[half, :, at] = jnp.broadcast_to(
                mean[:, half * 128 : (half + 1) * 128], (8, 128)
            )


def mix_kernel(entries, pert, centre, out):
    x = entries[...].astype(F32)
    tops, lows = separated(x[:, 0]), separated(x[:, 1])
    eye = jnp.where(iota((256, 256), 0) == iota((256, 256), 1), 1.0, 0.0)
    vectors, bounds, a1 = [], [], []
    for half in range(2):
        top, low = tops[half], lows[half]
        gram = jnp.concatenate(
            [top, jnp.concatenate([top[:, 128:].T, low[:, :128]], axis=1)], axis=0
        )
        vectors.append(
            jnp.concatenate(
                [low[:, 128:129] + low[:, 129:130], low[:, 130:131] + low[:, 131:132]], axis=0
            )
        )
        system = eye + gram * (1.0 / (MEMBERS - 1.0))
        sums = jnp.sum(jnp.abs(system), axis=1, keepdims=True)
        bound = jnp.max(sums, axis=0, keepdims=True)
        bounds.append(bound)
        a1.append(system / bound)
    s1 = [split(a) for a in a1]
    a2 = [product(s, s) for s in s1]
    s2 = [split(a) for a in a2]
    a3 = [product(s, t) for s, t in zip(s2, s1)]
    a4 = [product(s, s) for s in s2]
    z2 = [
        2.25 * eye - 2.4375 * a + 1.6875 * b - 0.5625 * c + 0.0625 * d
        for a, b, c, d in zip(a1, a2, a3, a4)
    ]
    t2 = [split(z) for z in z2]
    az = [split(product(s, t)) for s, t in zip(s1, t2)]
    zz = [split(product(t, t)) for t in t2]
    z3 = [1.5 * z - 0.5 * product(a, b) for z, a, b in zip(z2, az, zz)]
    for half in range(2):
        spread = z3[half] / jnp.sqrt(bounds[half])
        inner = jnp.sum(spread * vectors[half], axis=0, keepdims=True)
        shift = jnp.sum(spread * inner, axis=1, keepdims=True) / (MEMBERS - 1.0)
        mixing = (spread + shift).T.astype(BF16)
        result = dot(mixing, pert[half]) + centre[half][:1]
        for level in range(LEVELS):
            rows = result[:, level * 128 : (level + 1) * 128].reshape(PEERS, OWN, 128)
            out[:, level, :, half * 128 : (half + 1) * 128] = rows.astype(BF16)


def unpack_kernel(parts, out, sems):
    copies = [
        pltpu.make_async_copy(
            parts.at[peer], out.at[:, :, pl.ds(peer * COLS, COLS)], sems.at[peer]
        )
        for peer in range(PEERS)
    ]
    for copy in copies:
        copy.start()
    for copy in copies:
        copy.wait()


def swapped(value, first):
    pairs = []
    for i in range(first, lax.axis_size("region") - 1, 2):
        pairs += [(i, i + 1), (i + 1, i)]
    return lax.ppermute(value, "region", pairs)


def exchange(value):
    return lax.all_to_all(value, "member", split_axis=0, concat_axis=0, tiled=True)


def shape(*dims, dtype=BF16):
    return jax.ShapeDtypeStruct(dims, dtype)


CENTRED = (shape(2, MEMBERS, LEVELS * 128), shape(2, 8, LEVELS * 128, dtype=F32))


def on_device(
    background_trajectories,
    sensor_spread_matrix,
    departure_vector,
    inverse_error_variance,
    edge_tile_handoff,
    measurement_tile_table,
    distance_damping,
    active_tile_tally,
):
    val = departure_vector.reshape(HOME, 2, 128)
    wgt = inverse_error_variance.reshape(HOME, 2, 128)
    fields = background_trajectories.transpose(1, 0, 2)
    blocks = sensor_spread_matrix.reshape(OWN, HOME, OBS).transpose(1, 0, 2)
    me = lax.axis_index("member").reshape(1)

    region = lax.axis_index("region").reshape(1)
    about = (me, measurement_tile_table, distance_damping, active_tile_tally, val, wgt)

    def fields_first(fields, blocks, *about):
        packed = pl.pallas_call(
            pack_both_kernel,
            out_shape=shape(PEERS, LEVELS + 2, OWN, COLS),
            in_specs=[HBM, HBM],
            out_specs=ANY,
            scratch_shapes=[
                pltpu.VMEM((2, OWN, COLS), BF16),
                pltpu.SemaphoreType.DMA((2 * PEERS,)),
            ],
            compiler_params=PARAMS,
            name="pack_both",
        )(fields, blocks)
        gathered = exchange(packed)
        grams = pl.pallas_call(
            gram_kernel,
            out_shape=shape(PEERS, 2, 8, 256),
            in_specs=[SCALARS] * 4 + [WHOLE] * 3,
            out_specs=WHOLE,
            compiler_params=PARAMS,
            name="gram",
        )(*about, gathered)
        pert, centre = pl.pallas_call(
            centre_kernel,
            out_shape=CENTRED,
            in_specs=[WHOLE],
            out_specs=(WHOLE,) * 2,
            compiler_params=PARAMS,
            name="centre",
        )(gathered)
        return pert, centre, exchange(grams)

    def fields_second(fields, blocks, *about):
        packed = pl.pallas_call(
            pack_blocks_kernel,
            out_shape=shape(PEERS, 2, OWN, COLS),
            in_specs=[HBM],
            out_specs=ANY,
            scratch_shapes=[
                pltpu.VMEM((2, OWN, COLS), BF16),
                pltpu.SemaphoreType.DMA((PEERS,)),
            ],
            compiler_params=PARAMS,
            name="pack_blocks",
        )(blocks)
        grams = pl.pallas_call(
            gram_and_pack_kernel,
            out_shape=shape(PEERS, LEVELS + 2, OWN, COLS),
            in_specs=[SCALARS] * 4 + [WHOLE] * 3 + [HBM],
            out_specs=ANY,
            scratch_shapes=[
                pltpu.VMEM((PEERS, 2, 8, 256), BF16),
                pltpu.SemaphoreType.DMA((PEERS + 1,)),
            ],
            compiler_params=PARAMS,
            name="gram_and_pack",
        )(*about, exchange(packed), fields)
        return pl.pallas_call(
            centre_kernel,
            out_shape=CENTRED + (shape(PEERS, 2, 8, 256),),
            in_specs=[WHOLE],
            out_specs=(WHOLE,) * 3,
            compiler_params=PARAMS,
            name="centre_and_part",
        )(exchange(grams))

    even = lax.axis_index("region") % 2 == 0
    pert, centre, entries = lax.cond(even, fields_first, fields_second, fields, blocks, *about)

    across, within = pl.pallas_call(
        choose_kernel,
        out_shape=(shape(HANDED // 2, 2, 8, 256),) * 2,
        in_specs=[SCALARS, SCALARS, WHOLE],
        out_specs=(WHOLE, WHOLE),
        compiler_params=PARAMS,
        name="choose",
    )(region, edge_tile_handoff, entries)
    sums = pl.pallas_call(
        combine_kernel,
        out_shape=shape(PEERS, 2, 8, 256),
        in_specs=[SCALARS] + [WHOLE] * 3,
        out_specs=WHOLE,
        compiler_params=PARAMS,
        name="combine",
    )(region, entries, swapped(across, 1), swapped(within, 0))
    mixed = pl.pallas_call(
        mix_kernel,
        out_shape=shape(PEERS, LEVELS, OWN, COLS),
        in_specs=[WHOLE] * 3,
        out_specs=WHOLE,
        compiler_params=PARAMS,
        name="mix",
    )(exchange(sums), pert, centre)
    analysis = pl.pallas_call(
        unpack_kernel,
        out_shape=shape(LEVELS, OWN, PEERS * COLS),
        in_specs=[ANY],
        out_specs=HBM,
        scratch_shapes=[pltpu.SemaphoreType.DMA((PEERS,))],
        compiler_params=PARAMS,
        name="unpack",
    )(exchange(mixed))
    return analysis.transpose(1, 0, 2)


def solution(mesh):
    placed = (
        P("member", None, "region"),
        P("member", "region"),
        P("region"),
        P("region"),
        P(None, "region"),
        P(("region", "member"), None),
        P(("region", "member"), None),
        P(("region", "member")),
    )
    return jax.shard_map(
        on_device,
        mesh=mesh,
        in_specs=placed,
        out_specs=P("member", None, "region"),
        check_vma=False,
    )
```

```python
import jax
import jax.numpy as jnp
from jax import lax
from jax.experimental import pallas as pl
from jax.experimental.pallas import tpu as pltpu
from jax.sharding import PartitionSpec as P

F32 = jnp.float32
BF16 = jnp.bfloat16
MEMBERS = 256
PEERS = 32
OWN = 8
LEVELS = 6
OBS = 256
HANDED = 4
HOME = 56
EXT = 64
COLS = 256
MAXL = 16
VMEM_BYTES = 48 * 1024 * 1024
WHOLE = pl.BlockSpec(memory_space=pltpu.VMEM)
ANY = pl.BlockSpec(memory_space=pl.ANY)
HBM = pl.BlockSpec(memory_space=pltpu.HBM)
SCALARS = pl.BlockSpec(memory_space=pltpu.SMEM)
PARAMS = pltpu.CompilerParams(vmem_limit_bytes=VMEM_BYTES)


def iota(shape, dim):
    return lax.broadcasted_iota(jnp.int32, shape, dim)


def one_hot_lanes(shape):
    hit = iota(shape, 0) - 64 == (iota(shape, 1) >> 2)
    return jnp.where(hit, 1.0, 0.0).astype(BF16)


def dot(a, b):
    return jnp.dot(a, b, preferred_element_type=F32)


def split(a):
    high = a.astype(BF16)
    return high, (a - high.astype(F32)).astype(BF16)


def product(a, b):
    return dot(a[0], b[0]) + (dot(a[0], b[1]) + dot(a[1], b[0]))


def rounded(a):
    return a.astype(BF16).astype(F32)


def in_flight(pairs, sems):
    copies = [pltpu.make_async_copy(*ends, sems.at[k]) for k, ends in enumerate(pairs)]
    for copy in copies:
        copy.start()
    return copies


def landed(copies):
    for copy in copies:
        copy.wait()


def wide_row(pair):
    return jnp.concatenate([pair[:1], pair[1:]], axis=1)


def block_pairs(region, blocks, across, within, slots, out, group):
    odd = (region[0] & 1) == 1
    across = across[:HANDED].astype(F32)
    within = within[:HANDED].astype(F32)
    right = jnp.where(odd, across, within).astype(BF16)
    left = jnp.where(odd, within, across).astype(BF16)
    slots[: HANDED // 2] = right.reshape(HANDED // 2, 2, OWN, OBS)
    slots[HANDED // 2 :] = left.reshape(HANDED // 2, 2, OWN, OBS)
    return [
        (blocks, out.at[pl.ds(0, HOME // 2), pl.ds(group, 2)]),
        (slots, out.at[pl.ds(HOME // 2, HANDED), pl.ds(group, 2)]),
    ]


def field_pairs(fields, out):
    return [(fields.at[level], out.at[:, level]) for level in range(LEVELS)]


def pack_both_kernel(region, fields, blocks, across, within, out, slots, sems, field_sems):
    first = in_flight(field_pairs(fields, out), field_sems)
    pairs = block_pairs(region, blocks, across, within, slots, out, LEVELS)
    landed(first + in_flight(pairs, sems))


def pack_blocks_kernel(region, blocks, across, within, out, slots, sems):
    pairs = block_pairs(region, blocks, across, within, slots, out, 0)
    landed(in_flight(pairs, sems))


def first_half(rows):
    return iota(rows.shape, 1) < 4


def interleaved(first, second):
    first, second = (rows.reshape(16, 8, 256) for rows in (first, second))
    here = first_half(first)
    even = jnp.where(here, first, pltpu.roll(second, 4, 1))
    odd = jnp.where(here, pltpu.roll(first, 4, 1), second)
    return jnp.stack([even, odd], axis=1).reshape(PEERS, 8, 256)


def separated(rows):
    rows = rows.reshape(16, 2, 8, 256)
    even, odd = rows[:, 0], rows[:, 1]
    here = first_half(even)
    first = jnp.where(here, even, pltpu.roll(odd, 4, 1))
    second = jnp.where(here, pltpu.roll(even, 4, 1), odd)
    return first.reshape(128, 256), second.reshape(128, 256)


def grams_of(me, region, lists, val, wgt, across, within, gathered, group):
    lane = iota((128, 128), 1)
    row = iota((128, 128), 0) & 3
    top, low = [], []
    for half in range(2):
        slot = 2 * me[0] + half
        own = jnp.minimum(slot, HOME - 1)
        slot = jnp.maximum(slot - HOME, 0)
        from_right = jnp.where(slot < HANDED, 1, 0)
        place = HANDED + (slot & (HANDED - 1))
        handed = jnp.where(
            (region[0] & 1) == from_right,
            across[place].astype(F32),
            within[place].astype(F32),
        )
        is_own = 2 * me[0] + half < HOME
        w = jnp.where(is_own, wide_row(wgt[own]), handed[0:1] + handed[1:2])
        v = jnp.where(is_own, wide_row(val[own]), handed[2:3] + handed[3:4])
        y = gathered[:, group + half].astype(F32).reshape(MEMBERS, OBS)
        scaled = (y * w).astype(BF16)
        gram = lax.dot_general(
            y.astype(BF16), scaled, (((1,), (1,)), ((), ())), preferred_element_type=F32
        )
        vector = jnp.sum(y * (w * v), axis=1, keepdims=True)
        vector_high = rounded(vector)
        vector_low = vector - vector_high
        coeff = lists[8 * half : 8 * half + 1]
        coeff_high = rounded(coeff)
        extra = jnp.where(row == 0, coeff_high, jnp.where(row == 1, coeff - coeff_high, 0.0))
        for place, column in enumerate(
            (vector_high[:128], vector_low[:128], vector_high[128:], vector_low[128:])
        ):
            extra = jnp.where(lane == place, column, extra)
        top.append(gram[:128, :])
        low.append(jnp.concatenate([gram[128:, 128:], extra], axis=1))
    return interleaved(*top).astype(BF16), interleaved(*low).astype(BF16)


def gram_kernel(*refs):
    *about, gathered, out = refs
    out[:, 0], out[:, 1] = grams_of(*about, gathered, gathered.shape[1] - 2)


def pick_kernel(region, chosen, blocks, val, wgt, across, within, vals, wgts, sems):
    odd = region[0] & 1
    sides = ((1 - odd, across), (odd, within))
    pairs = [(val, vals), (wgt, wgts)]
    for side, out in sides:
        for k in range(HANDED):
            pairs.append((blocks.at[chosen[side, k]], out.at[k]))
    landed(in_flight(pairs, sems))
    row = iota((OWN, OBS), 0)
    for side, out in sides:
        for k in range(HANDED):
            block = chosen[side, k]
            w, v = wide_row(wgts[block]), wide_row(vals[block])
            w_high, v_high = rounded(w), rounded(v)
            tail = jnp.where(row == 2, v_high, jnp.where(row == 3, v - v_high, 0.0))
            tail = jnp.where(row == 0, w_high, jnp.where(row == 1, w - w_high, tail))
            out[HANDED + k] = tail.astype(BF16)


def lists_kernel(table, damping, tally, out):
    slot_of_lane = iota((1, 128), 1) - 64
    for half in range(2):
        coeff = jnp.zeros((1, 128), F32)
        for position in range(MAXL):
            used = jnp.where(position < tally[half], damping[half, position], 0.0)
            slot = (table[half, position] - HANDED) & (EXT - 1)
            coeff = coeff + jnp.where(slot_of_lane == slot, used, 0.0)
        out[half * 8 : (half + 1) * 8] = jnp.broadcast_to(coeff, (8, 128))


def sums_of(x):
    coeffs = x[:, 1, :, 128:]
    here = first_half(coeffs)
    high = jnp.where(here, coeffs[:, 0:1], coeffs[:, 4:5]).reshape(256, 128)
    low = jnp.where(here, coeffs[:, 1:2], coeffs[:, 5:6]).reshape(256, 128)
    spread_out = one_hot_lanes((128, 256))
    wide = dot(jnp.concatenate([high, low], axis=0).astype(BF16), spread_out)
    same = ((iota((256, 256), 0) ^ iota((256, 256), 1)) & 3) == 0
    high = jnp.where(same, wide[:256], 0.0).astype(BF16)
    low = jnp.where(same, wide[256:], 0.0).astype(BF16)
    total = []
    for part in range(2):
        rows = x[:, part].reshape(256, 256).astype(BF16)
        total.append(dot(high, rows) + dot(low, rows))
    tail = total[1][:, 128:]
    both = tail + pltpu.roll(tail, 127, 1)
    high = rounded(both)
    low = pltpu.roll(both - high, 1, 1)
    lane = iota((256, 128), 1)
    tail = jnp.where(lane < 4, jnp.where((lane & 1) == 0, high, low), tail)
    tail = jnp.concatenate([total[1][:, :128], tail], axis=1)
    return (rows.reshape(PEERS, 8, 256).astype(BF16) for rows in (total[0], tail))


def combine_kernel(entries, fields, out, pert, centre):
    centre_kernel(fields, pert, centre)
    out[:, 0], out[:, 1] = sums_of(entries[...].astype(F32))


def combine_and_pack_kernel(entries, fields, out, part, sems):
    copies = in_flight(field_pairs(fields, out), sems)
    part[:, 0], part[:, 1] = sums_of(entries[...].astype(F32))
    last = pltpu.make_async_copy(part, out.at[:, pl.ds(LEVELS, 2)], sems.at[LEVELS])
    last.start()
    landed(copies)
    last.wait()


def centre_kernel(fields, pert, centre, entries=None):
    if entries is not None:
        entries[...] = fields[:, LEVELS:]
    for level in range(LEVELS):
        x = fields[:, level].astype(F32).reshape(MEMBERS, COLS)
        mean = jnp.sum(x, axis=0, keepdims=True) / MEMBERS
        away = (x - mean).astype(BF16)
        for half in range(2):
            at = slice(level * 128, (level + 1) * 128)
            pert[half, :, at] = away[:, half * 128 : (half + 1) * 128]
            centre[half, :, at] = jnp.broadcast_to(
                mean[:, half * 128 : (half + 1) * 128], (8, 128)
            )


def mix_kernel(entries, pert, centre, out):
    x = entries[...].astype(F32)
    tops, lows = separated(x[:, 0]), separated(x[:, 1])
    eye = jnp.where(iota((256, 256), 0) == iota((256, 256), 1), 1.0, 0.0)
    vectors, bounds, a1 = [], [], []
    for half in range(2):
        top, low = tops[half], lows[half]
        gram = jnp.concatenate(
            [top, jnp.concatenate([top[:, 128:].T, low[:, :128]], axis=1)], axis=0
        )
        vectors.append(
            jnp.concatenate(
                [low[:, 128:129] + low[:, 129:130], low[:, 130:131] + low[:, 131:132]], axis=0
            )
        )
        system = eye + gram * (1.0 / (MEMBERS - 1.0))
        sums = jnp.sum(jnp.abs(system), axis=1, keepdims=True)
        bound = jnp.max(sums, axis=0, keepdims=True)
        bounds.append(bound)
        a1.append(system / bound)
    s1 = [split(a) for a in a1]
    a2 = [product(s, s) for s in s1]
    s2 = [split(a) for a in a2]
    a3 = [product(s, t) for s, t in zip(s2, s1)]
    a4 = [product(s, s) for s in s2]
    z2 = [
        2.25 * eye - 2.4375 * a + 1.6875 * b - 0.5625 * c + 0.0625 * d
        for a, b, c, d in zip(a1, a2, a3, a4)
    ]
    t2 = [split(z) for z in z2]
    az = [split(product(s, t)) for s, t in zip(s1, t2)]
    zz = [split(product(t, t)) for t in t2]
    z3 = [1.5 * z - 0.5 * product(a, b) for z, a, b in zip(z2, az, zz)]
    for half in range(2):
        spread = z3[half] / jnp.sqrt(bounds[half])
        inner = jnp.sum(spread * vectors[half], axis=0, keepdims=True)
        shift = jnp.sum(spread * inner, axis=1, keepdims=True) / (MEMBERS - 1.0)
        mixing = (spread + shift).T.astype(BF16)
        result = dot(mixing, pert[half]) + centre[half][:1]
        for level in range(LEVELS):
            rows = result[:, level * 128 : (level + 1) * 128].reshape(PEERS, OWN, 128)
            out[:, level, :, half * 128 : (half + 1) * 128] = rows.astype(BF16)


def unpack_kernel(parts, out, sems):
    landed(in_flight([(parts.at[:, level], out.at[level]) for level in range(LEVELS)], sems))


def swapped(value, first):
    pairs = []
    for i in range(first, lax.axis_size("region") - 1, 2):
        pairs += [(i, i + 1), (i + 1, i)]
    return lax.ppermute(value, "region", pairs)


def exchange(value):
    return lax.all_to_all(value, "member", split_axis=0, concat_axis=0, tiled=True)


def shape(*dims, dtype=BF16):
    return jax.ShapeDtypeStruct(dims, dtype)


CENTRED = (shape(2, MEMBERS, LEVELS * 128), shape(2, 8, LEVELS * 128, dtype=F32))


WITH_FIELDS = [pltpu.VMEM((PEERS, 2, 8, 256), BF16), pltpu.SemaphoreType.DMA((LEVELS + 1,))]


def on_device(
    background_trajectories,
    sensor_spread_matrix,
    departure_vector,
    inverse_error_variance,
    edge_tile_handoff,
    measurement_tile_table,
    distance_damping,
    active_tile_tally,
):
    val = departure_vector.reshape(HOME, 2, 128)
    wgt = inverse_error_variance.reshape(HOME, 2, 128)
    fields = background_trajectories.reshape(OWN, LEVELS, PEERS, COLS).transpose(1, 2, 0, 3)
    blocks = sensor_spread_matrix.reshape(OWN, HOME, OBS).transpose(1, 0, 2)
    me = lax.axis_index("member").reshape(1)

    region = lax.axis_index("region").reshape(1)
    lists = pl.pallas_call(
        lists_kernel,
        out_shape=shape(16, 128, dtype=F32),
        in_specs=[SCALARS] * 3,
        out_specs=WHOLE,
        compiler_params=PARAMS,
        name="lists",
    )(measurement_tile_table, distance_damping, active_tile_tally)

    across, within = pl.pallas_call(
        pick_kernel,
        out_shape=(shape(2 * HANDED, OWN, OBS),) * 2,
        in_specs=[SCALARS, SCALARS, HBM, HBM, HBM],
        out_specs=(WHOLE, WHOLE),
        scratch_shapes=[
            pltpu.VMEM((HOME, 2, 128), F32),
            pltpu.VMEM((HOME, 2, 128), F32),
            pltpu.SemaphoreType.DMA((2 * HANDED + 2,)),
        ],
        compiler_params=PARAMS,
        name="pick",
    )(region, edge_tile_handoff, blocks, val, wgt)
    across = swapped(across, 1)
    within = swapped(within, 0)

    def gram(gathered, *about):
        return pl.pallas_call(
            gram_kernel,
            out_shape=shape(PEERS, 2, 8, 256),
            in_specs=[SCALARS] * 2 + [WHOLE] * 6,
            out_specs=WHOLE,
            compiler_params=PARAMS,
            name="gram",
        )(*about, gathered)

    def fields_first(fields, blocks, *about):
        _, region, *_, across, within = about
        packed = pl.pallas_call(
            pack_both_kernel,
            out_shape=shape(PEERS, LEVELS + 2, OWN, COLS),
            in_specs=[SCALARS, HBM, HBM, WHOLE, WHOLE],
            out_specs=ANY,
            scratch_shapes=[
                pltpu.VMEM((HANDED, 2, OWN, COLS), BF16),
                pltpu.SemaphoreType.DMA((2,)),
                pltpu.SemaphoreType.DMA((LEVELS,)),
            ],
            compiler_params=PARAMS,
            name="pack_both",
        )(region, fields, blocks, across, within)
        gathered = exchange(packed)
        grams = exchange(gram(gathered, *about))
        sums, pert, centre = pl.pallas_call(
            combine_kernel,
            out_shape=(shape(PEERS, 2, 8, 256),) + CENTRED,
            in_specs=[WHOLE] * 2,
            out_specs=(WHOLE,) * 3,
            compiler_params=PARAMS,
            name="combine",
        )(grams, gathered)
        return pert, centre, exchange(sums)

    def fields_last(fields, blocks, *about):
        _, region, *_, across, within = about
        packed = pl.pallas_call(
            pack_blocks_kernel,
            out_shape=shape(PEERS, 2, OWN, COLS),
            in_specs=[SCALARS, HBM, WHOLE, WHOLE],
            out_specs=ANY,
            scratch_shapes=[
                pltpu.VMEM((HANDED, 2, OWN, COLS), BF16),
                pltpu.SemaphoreType.DMA((2,)),
            ],
            compiler_params=PARAMS,
            name="pack_blocks",
        )(region, blocks, across, within)
        grams = exchange(gram(exchange(packed), *about))
        sums = pl.pallas_call(
            combine_and_pack_kernel,
            out_shape=shape(PEERS, LEVELS + 2, OWN, COLS),
            in_specs=[WHOLE, HBM],
            out_specs=ANY,
            scratch_shapes=WITH_FIELDS,
            compiler_params=PARAMS,
            name="combine_and_pack",
        )(grams, fields)
        return pl.pallas_call(
            centre_kernel,
            out_shape=CENTRED + (shape(PEERS, 2, 8, 256),),
            in_specs=[WHOLE],
            out_specs=(WHOLE,) * 3,
            compiler_params=PARAMS,
            name="centre_and_part",
        )(exchange(sums))

    even = lax.axis_index("region") % 2 == 0
    about = (me, region, lists, val, wgt, across, within)
    pert, centre, systems = lax.cond(
        even,
        fields_first,
        fields_last,
        fields,
        blocks.reshape(HOME // 2, 2, OWN, OBS),
        *about,
    )

    mixed = pl.pallas_call(
        mix_kernel,
        out_shape=shape(PEERS, LEVELS, OWN, COLS),
        in_specs=[WHOLE] * 3,
        out_specs=WHOLE,
        compiler_params=PARAMS,
        name="mix",
    )(systems, pert, centre)
    analysis = pl.pallas_call(
        unpack_kernel,
        out_shape=shape(LEVELS, PEERS, OWN, COLS),
        in_specs=[ANY],
        out_specs=HBM,
        scratch_shapes=[pltpu.SemaphoreType.DMA((LEVELS,))],
        compiler_params=PARAMS,
        name="unpack",
    )(exchange(mixed))
    return analysis.transpose(2, 0, 1, 3).reshape(OWN, LEVELS, PEERS * COLS)


def solution(mesh):
    placed = (
        P("member", None, "region"),
        P("member", "region"),
        P("region"),
        P("region"),
        P(None, "region"),
        P(("region", "member"), None),
        P(("region", "member"), None),
        P(("region", "member")),
    )
    return jax.shard_map(
        on_device,
        mesh=mesh,
        in_specs=placed,
        out_specs=P("member", None, "region"),
        check_vma=False,
    )
```

```python
import jax
import jax.numpy as jnp
from jax import lax
from jax.experimental import pallas as pl
from jax.experimental.pallas import tpu as pltpu
from jax.sharding import PartitionSpec as P

F32 = jnp.float32
BF16 = jnp.bfloat16
MEMBERS = 256
PEERS = 32
OWN = 8
LEVELS = 6
OBS = 256
HANDED = 4
HOME = 56
EXT = 64
COLS = 256
MAXL = 16
VMEM_BYTES = 48 * 1024 * 1024
WHOLE = pl.BlockSpec(memory_space=pltpu.VMEM)
ANY = pl.BlockSpec(memory_space=pl.ANY)
HBM = pl.BlockSpec(memory_space=pltpu.HBM)
SCALARS = pl.BlockSpec(memory_space=pltpu.SMEM)
PARAMS = pltpu.CompilerParams(vmem_limit_bytes=VMEM_BYTES)


def iota(shape, dim):
    return lax.broadcasted_iota(jnp.int32, shape, dim)


def one_hot_lanes(shape):
    hit = iota(shape, 0) - 64 == (iota(shape, 1) >> 2)
    return jnp.where(hit, 1.0, 0.0).astype(BF16)


def dot(a, b):
    return jnp.dot(a, b, preferred_element_type=F32)


def split(a):
    high = a.astype(BF16)
    return high, (a - high.astype(F32)).astype(BF16)


def product(a, b):
    left = jnp.concatenate([a[0], a[0], a[1]], axis=1)
    return dot(left, jnp.concatenate([b[0], b[1], b[0]], axis=0))


def rounded(a):
    return a.astype(BF16).astype(F32)


def in_flight(pairs, sems):
    copies = [pltpu.make_async_copy(*ends, sems.at[k]) for k, ends in enumerate(pairs)]
    for copy in copies:
        copy.start()
    return copies


def landed(copies):
    for copy in copies:
        copy.wait()


def wide_row(pair):
    return jnp.concatenate([pair[:1], pair[1:]], axis=1)


def block_pairs(region, blocks, across, within, slots, out, group):
    odd = (region[0] & 1) == 1
    across = across[:HANDED].astype(F32)
    within = within[:HANDED].astype(F32)
    right = jnp.where(odd, across, within).astype(BF16)
    left = jnp.where(odd, within, across).astype(BF16)
    slots[: HANDED // 2] = right.reshape(HANDED // 2, 2, OWN, OBS)
    slots[HANDED // 2 :] = left.reshape(HANDED // 2, 2, OWN, OBS)
    return [
        (blocks, out.at[pl.ds(0, HOME // 2), pl.ds(group, 2)]),
        (slots, out.at[pl.ds(HOME // 2, HANDED), pl.ds(group, 2)]),
    ]


def field_pairs(fields, out):
    return [(fields.at[level], out.at[:, level]) for level in range(LEVELS)]


def pack_both_kernel(region, fields, blocks, across, within, out, slots, sems, field_sems):
    first = in_flight(field_pairs(fields, out), field_sems)
    pairs = block_pairs(region, blocks, across, within, slots, out, LEVELS)
    landed(first + in_flight(pairs, sems))


def pack_blocks_kernel(region, blocks, across, within, out, slots, sems):
    pairs = block_pairs(region, blocks, across, within, slots, out, 0)
    landed(in_flight(pairs, sems))


def first_half(rows):
    return iota(rows.shape, 1) < 4


def interleaved(first, second):
    first, second = (rows.reshape(16, 8, 256) for rows in (first, second))
    here = first_half(first)
    even = jnp.where(here, first, pltpu.roll(second, 4, 1))
    odd = jnp.where(here, pltpu.roll(first, 4, 1), second)
    return jnp.stack([even, odd], axis=1).reshape(PEERS, 8, 256)


def separated(rows):
    rows = rows.reshape(16, 2, 8, 256)
    even, odd = rows[:, 0], rows[:, 1]
    here = first_half(even)
    first = jnp.where(here, even, pltpu.roll(odd, 4, 1))
    second = jnp.where(here, pltpu.roll(even, 4, 1), odd)
    return first.reshape(128, 256), second.reshape(128, 256)


def grams_of(me, region, lists, val, wgt, across, within, gathered, group):
    lane = iota((128, 128), 1)
    row = iota((128, 128), 0) & 3
    top, low = [], []
    for half in range(2):
        slot = 2 * me[0] + half
        own = jnp.minimum(slot, HOME - 1)
        slot = jnp.maximum(slot - HOME, 0)
        from_right = jnp.where(slot < HANDED, 1, 0)
        place = HANDED + (slot & (HANDED - 1))
        handed = jnp.where(
            (region[0] & 1) == from_right,
            across[place].astype(F32),
            within[place].astype(F32),
        )
        is_own = 2 * me[0] + half < HOME
        w = jnp.where(is_own, wide_row(wgt[own]), handed[0:1] + handed[1:2])
        v = jnp.where(is_own, wide_row(val[own]), handed[2:3] + handed[3:4])
        y = gathered[:, group + half].astype(F32).reshape(MEMBERS, OBS)
        scaled = (y * w).astype(BF16)
        gram = lax.dot_general(
            y.astype(BF16), scaled, (((1,), (1,)), ((), ())), preferred_element_type=F32
        )
        vector = jnp.sum(y * (w * v), axis=1, keepdims=True)
        vector_high = rounded(vector)
        vector_low = vector - vector_high
        coeff = lists[8 * half : 8 * half + 1]
        coeff_high = rounded(coeff)
        extra = jnp.where(row == 0, coeff_high, jnp.where(row == 1, coeff - coeff_high, 0.0))
        for place, column in enumerate(
            (vector_high[:128], vector_low[:128], vector_high[128:], vector_low[128:])
        ):
            extra = jnp.where(lane == place, column, extra)
        top.append(gram[:128, :])
        low.append(jnp.concatenate([gram[128:, 128:], extra], axis=1))
    return interleaved(*top).astype(BF16), interleaved(*low).astype(BF16)


def gram_kernel(*refs):
    *about, gathered, out = refs
    out[:, 0], out[:, 1] = grams_of(*about, gathered, gathered.shape[1] - 2)


def pick_kernel(region, chosen, blocks, val, wgt, across, within, held, vals, wgts, sems):
    odd = region[0] & 1
    sides = ((1 - odd, across), (odd, within))
    landed(in_flight([(blocks, held), (val, vals), (wgt, wgts)], sems))
    row = iota((OWN, OBS), 0)
    for side, out in sides:
        for k in range(HANDED):
            block = chosen[side, k]
            out[k] = held[block]
            w, v = wide_row(wgts[block]), wide_row(vals[block])
            w_high, v_high = rounded(w), rounded(v)
            tail = jnp.where(row == 2, v_high, jnp.where(row == 3, v - v_high, 0.0))
            tail = jnp.where(row == 0, w_high, jnp.where(row == 1, w - w_high, tail))
            out[HANDED + k] = tail.astype(BF16)


def lists_kernel(table, damping, tally, out):
    slot_of_lane = iota((1, 128), 1) - 64
    for half in range(2):
        coeff = jnp.zeros((1, 128), F32)
        for position in range(MAXL):
            used = jnp.where(position < tally[half], damping[half, position], 0.0)
            slot = (table[half, position] - HANDED) & (EXT - 1)
            coeff = coeff + jnp.where(slot_of_lane == slot, used, 0.0)
        out[half * 8 : (half + 1) * 8] = jnp.broadcast_to(coeff, (8, 128))


def sums_of(x):
    coeffs = x[:, 1, :, 128:]
    here = first_half(coeffs)
    high = jnp.where(here, coeffs[:, 0:1], coeffs[:, 4:5]).reshape(256, 128)
    low = jnp.where(here, coeffs[:, 1:2], coeffs[:, 5:6]).reshape(256, 128)
    spread_out = one_hot_lanes((128, 256))
    wide = dot(jnp.concatenate([high, low], axis=0).astype(BF16), spread_out)
    same = ((iota((256, 256), 0) ^ iota((256, 256), 1)) & 3) == 0
    high = jnp.where(same, wide[:256], 0.0).astype(BF16)
    low = jnp.where(same, wide[256:], 0.0).astype(BF16)
    total = []
    for part in range(2):
        rows = x[:, part].reshape(256, 256).astype(BF16)
        total.append(dot(high, rows) + dot(low, rows))
    tail = total[1][:, 128:]
    both = tail + pltpu.roll(tail, 127, 1)
    high = rounded(both)
    low = pltpu.roll(both - high, 1, 1)
    lane = iota((256, 128), 1)
    tail = jnp.where(lane < 4, jnp.where((lane & 1) == 0, high, low), tail)
    tail = jnp.concatenate([total[1][:, :128], tail], axis=1)
    return (rows.reshape(PEERS, 8, 256).astype(BF16) for rows in (total[0], tail))


def combine_kernel(entries, fields, out, pert, centre):
    centre_kernel(fields, pert, centre)
    out[:, 0], out[:, 1] = sums_of(entries[...].astype(F32))


def combine_and_pack_kernel(entries, fields, out, part, sems):
    copies = in_flight(field_pairs(fields, out), sems)
    part[:, 0], part[:, 1] = sums_of(entries[...].astype(F32))
    last = pltpu.make_async_copy(part, out.at[:, pl.ds(LEVELS, 2)], sems.at[LEVELS])
    last.start()
    landed(copies)
    last.wait()


def centre_kernel(fields, pert, centre, entries=None):
    if entries is not None:
        entries[...] = fields[:, LEVELS:]
    for level in range(LEVELS):
        x = fields[:, level].astype(F32).reshape(MEMBERS, COLS)
        mean = jnp.sum(x, axis=0, keepdims=True) / MEMBERS
        away = (x - mean).astype(BF16)
        for half in range(2):
            at = slice(level * 128, (level + 1) * 128)
            pert[half, :, at] = away[:, half * 128 : (half + 1) * 128]
            centre[half, :, at] = jnp.broadcast_to(
                mean[:, half * 128 : (half + 1) * 128], (8, 128)
            )


def mix_kernel(entries, pert, centre, out):
    x = entries[...].astype(F32)
    tops, lows = separated(x[:, 0]), separated(x[:, 1])
    eye = jnp.where(iota((256, 256), 0) == iota((256, 256), 1), 1.0, 0.0)
    vectors, bounds, a1 = [], [], []
    for half in range(2):
        top, low = tops[half], lows[half]
        gram = jnp.concatenate(
            [top, jnp.concatenate([top[:, 128:].T, low[:, :128]], axis=1)], axis=0
        )
        vectors.append(
            jnp.concatenate(
                [low[:, 128:129] + low[:, 129:130], low[:, 130:131] + low[:, 131:132]], axis=0
            )
        )
        system = eye + gram * (1.0 / (MEMBERS - 1.0))
        sums = jnp.sum(jnp.abs(system), axis=1, keepdims=True)
        bound = jnp.max(sums, axis=0, keepdims=True)
        bounds.append(bound)
        a1.append(system / bound)
    s1 = [split(a) for a in a1]
    a2 = [product(s, s) for s in s1]
    s2 = [split(a) for a in a2]
    a3 = [product(s, t) for s, t in zip(s2, s1)]
    a4 = [product(s, s) for s in s2]
    z2 = [
        2.25 * eye - 2.4375 * a + 1.6875 * b - 0.5625 * c + 0.0625 * d
        for a, b, c, d in zip(a1, a2, a3, a4)
    ]
    t2 = [split(z) for z in z2]
    az = [split(product(s, t)) for s, t in zip(s1, t2)]
    zz = [split(product(t, t)) for t in t2]
    z3 = [1.5 * z - 0.5 * product(a, b) for z, a, b in zip(z2, az, zz)]
    for half in range(2):
        spread = z3[half] / jnp.sqrt(bounds[half])
        across = jnp.sum(eye * vectors[half], axis=0, keepdims=True)
        inner = jnp.sum(spread * across, axis=1, keepdims=True)
        shift = jnp.sum(spread * inner, axis=0, keepdims=True) / (MEMBERS - 1.0)
        mixing = (spread + shift).astype(BF16)
        result = dot(mixing, pert[half]) + centre[half][:1]
        for level in range(LEVELS):
            rows = result[:, level * 128 : (level + 1) * 128].reshape(PEERS, OWN, 128)
            out[:, level, :, half * 128 : (half + 1) * 128] = rows.astype(BF16)


def unpack_kernel(parts, out, sems):
    landed(in_flight([(parts.at[:, level], out.at[level]) for level in range(LEVELS)], sems))


def swapped(value, first):
    pairs = []
    for i in range(first, lax.axis_size("region") - 1, 2):
        pairs += [(i, i + 1), (i + 1, i)]
    return lax.ppermute(value, "region", pairs)


def exchange(value):
    return lax.all_to_all(value, "member", split_axis=0, concat_axis=0, tiled=True)


def shape(*dims, dtype=BF16):
    return jax.ShapeDtypeStruct(dims, dtype)


CENTRED = (shape(2, MEMBERS, LEVELS * 128), shape(2, 8, LEVELS * 128, dtype=F32))


WITH_FIELDS = [pltpu.VMEM((PEERS, 2, 8, 256), BF16), pltpu.SemaphoreType.DMA((LEVELS + 1,))]


def on_device(
    background_trajectories,
    sensor_spread_matrix,
    departure_vector,
    inverse_error_variance,
    edge_tile_handoff,
    measurement_tile_table,
    distance_damping,
    active_tile_tally,
):
    val = departure_vector.reshape(HOME, 2, 128)
    wgt = inverse_error_variance.reshape(HOME, 2, 128)
    fields = background_trajectories.reshape(OWN, LEVELS, PEERS, COLS).transpose(1, 2, 0, 3)
    blocks = sensor_spread_matrix.reshape(OWN, HOME, OBS).transpose(1, 0, 2)
    me = lax.axis_index("member").reshape(1)

    region = lax.axis_index("region").reshape(1)
    lists = pl.pallas_call(
        lists_kernel,
        out_shape=shape(16, 128, dtype=F32),
        in_specs=[SCALARS] * 3,
        out_specs=WHOLE,
        compiler_params=PARAMS,
        name="lists",
    )(measurement_tile_table, distance_damping, active_tile_tally)

    across, within = pl.pallas_call(
        pick_kernel,
        out_shape=(shape(2 * HANDED, OWN, OBS),) * 2,
        in_specs=[SCALARS, SCALARS, HBM, HBM, HBM],
        out_specs=(WHOLE, WHOLE),
        scratch_shapes=[
            pltpu.VMEM((HOME, OWN, OBS), BF16),
            pltpu.VMEM((HOME, 2, 128), F32),
            pltpu.VMEM((HOME, 2, 128), F32),
            pltpu.SemaphoreType.DMA((3,)),
        ],
        compiler_params=PARAMS,
        name="pick",
    )(region, edge_tile_handoff, blocks, val, wgt)
    across = swapped(across, 1)
    within = swapped(within, 0)

    def gram(gathered, *about):
        return pl.pallas_call(
            gram_kernel,
            out_shape=shape(PEERS, 2, 8, 256),
            in_specs=[SCALARS] * 2 + [WHOLE] * 6,
            out_specs=WHOLE,
            compiler_params=PARAMS,
            name="gram",
        )(*about, gathered)

    def fields_first(fields, blocks, *about):
        _, region, *_, across, within = about
        packed = pl.pallas_call(
            pack_both_kernel,
            out_shape=shape(PEERS, LEVELS + 2, OWN, COLS),
            in_specs=[SCALARS, HBM, HBM, WHOLE, WHOLE],
            out_specs=ANY,
            scratch_shapes=[
                pltpu.VMEM((HANDED, 2, OWN, COLS), BF16),
                pltpu.SemaphoreType.DMA((2,)),
                pltpu.SemaphoreType.DMA((LEVELS,)),
            ],
            compiler_params=PARAMS,
            name="pack_both",
        )(region, fields, blocks, across, within)
        gathered = exchange(packed)
        grams = exchange(gram(gathered, *about))
        sums, pert, centre = pl.pallas_call(
            combine_kernel,
            out_shape=(shape(PEERS, 2, 8, 256),) + CENTRED,
            in_specs=[WHOLE] * 2,
            out_specs=(WHOLE,) * 3,
            compiler_params=PARAMS,
            name="combine",
        )(grams, gathered)
        return pert, centre, exchange(sums)

    def fields_last(fields, blocks, *about):
        _, region, *_, across, within = about
        packed = pl.pallas_call(
            pack_blocks_kernel,
            out_shape=shape(PEERS, 2, OWN, COLS),
            in_specs=[SCALARS, HBM, WHOLE, WHOLE],
            out_specs=ANY,
            scratch_shapes=[
                pltpu.VMEM((HANDED, 2, OWN, COLS), BF16),
                pltpu.SemaphoreType.DMA((2,)),
            ],
            compiler_params=PARAMS,
            name="pack_blocks",
        )(region, blocks, across, within)
        grams = exchange(gram(exchange(packed), *about))
        sums = pl.pallas_call(
            combine_and_pack_kernel,
            out_shape=shape(PEERS, LEVELS + 2, OWN, COLS),
            in_specs=[WHOLE, HBM],
            out_specs=ANY,
            scratch_shapes=WITH_FIELDS,
            compiler_params=PARAMS,
            name="combine_and_pack",
        )(grams, fields)
        return pl.pallas_call(
            centre_kernel,
            out_shape=CENTRED + (shape(PEERS, 2, 8, 256),),
            in_specs=[WHOLE],
            out_specs=(WHOLE,) * 3,
            compiler_params=PARAMS,
            name="centre_and_part",
        )(exchange(sums))

    even = lax.axis_index("region") % 2 == 0
    about = (me, region, lists, val, wgt, across, within)
    pert, centre, systems = lax.cond(
        even,
        fields_first,
        fields_last,
        fields,
        blocks.reshape(HOME // 2, 2, OWN, OBS),
        *about,
    )

    mixed = pl.pallas_call(
        mix_kernel,
        out_shape=shape(PEERS, LEVELS, OWN, COLS),
        in_specs=[WHOLE] * 3,
        out_specs=WHOLE,
        compiler_params=PARAMS,
        name="mix",
    )(systems, pert, centre)
    analysis = pl.pallas_call(
        unpack_kernel,
        out_shape=shape(LEVELS, PEERS, OWN, COLS),
        in_specs=[ANY],
        out_specs=HBM,
        scratch_shapes=[pltpu.SemaphoreType.DMA((LEVELS,))],
        compiler_params=PARAMS,
        name="unpack",
    )(exchange(mixed))
    return analysis.transpose(2, 0, 1, 3).reshape(OWN, LEVELS, PEERS * COLS)


def solution(mesh):
    placed = (
        P("member", None, "region"),
        P("member", "region"),
        P("region"),
        P("region"),
        P(None, "region"),
        P(("region", "member"), None),
        P(("region", "member"), None),
        P(("region", "member")),
    )
    return jax.shard_map(
        on_device,
        mesh=mesh,
        in_specs=placed,
        out_specs=P("member", None, "region"),
        check_vma=False,
    )
```

```python
import jax
import jax.numpy as jnp
from jax import lax
from jax.experimental import pallas as pl
from jax.experimental.pallas import tpu as pltpu
from jax.sharding import PartitionSpec as P

F32 = jnp.float32
BF16 = jnp.bfloat16
MEMBERS = 256
PEERS = 32
OWN = 8
LEVELS = 6
OBS = 256
HANDED = 4
HOME = 56
EXT = 64
COLS = 256
MAXL = 16
VMEM_BYTES = 48 * 1024 * 1024
WHOLE = pl.BlockSpec(memory_space=pltpu.VMEM)
ANY = pl.BlockSpec(memory_space=pl.ANY)
HBM = pl.BlockSpec(memory_space=pltpu.HBM)
SCALARS = pl.BlockSpec(memory_space=pltpu.SMEM)
PARAMS = pltpu.CompilerParams(vmem_limit_bytes=VMEM_BYTES)


def iota(shape, dim):
    return lax.broadcasted_iota(jnp.int32, shape, dim)


def one_hot_lanes(shape):
    hit = iota(shape, 0) - 64 == (iota(shape, 1) >> 2)
    return jnp.where(hit, 1.0, 0.0).astype(BF16)


def dot(a, b):
    return jnp.dot(a, b, preferred_element_type=F32)


def split(a):
    high = a.astype(BF16)
    return high, (a - high.astype(F32)).astype(BF16)


def single(a, b):
    return dot(a.astype(BF16), b.astype(BF16))


def product(a, b):
    left = jnp.concatenate([a[0], a[0], a[1]], axis=1)
    return dot(left, jnp.concatenate([b[0], b[1], b[0]], axis=0))


def rounded(a):
    return a.astype(BF16).astype(F32)


def in_flight(pairs, sems):
    copies = [pltpu.make_async_copy(*ends, sems.at[k]) for k, ends in enumerate(pairs)]
    for copy in copies:
        copy.start()
    return copies


def landed(copies):
    for copy in copies:
        copy.wait()


def wide_row(pair):
    return jnp.concatenate([pair[:1], pair[1:]], axis=1)


def block_pairs(region, blocks, across, within, slots, out, group):
    odd = (region[0] & 1) == 1
    across = across[:HANDED].astype(F32)
    within = within[:HANDED].astype(F32)
    right = jnp.where(odd, across, within).astype(BF16)
    left = jnp.where(odd, within, across).astype(BF16)
    slots[: HANDED // 2] = right.reshape(HANDED // 2, 2, OWN, OBS)
    slots[HANDED // 2 :] = left.reshape(HANDED // 2, 2, OWN, OBS)
    return [
        (blocks, out.at[pl.ds(0, HOME // 2), pl.ds(group, 2)]),
        (slots, out.at[pl.ds(HOME // 2, HANDED), pl.ds(group, 2)]),
    ]


def field_pairs(fields, out):
    return [(fields.at[level], out.at[:, level]) for level in range(LEVELS)]


def pack_both_kernel(region, fields, blocks, across, within, out, slots, sems, field_sems):
    first = in_flight(field_pairs(fields, out), field_sems)
    pairs = block_pairs(region, blocks, across, within, slots, out, LEVELS)
    landed(first + in_flight(pairs, sems))


def pack_blocks_kernel(region, blocks, across, within, out, slots, sems):
    pairs = block_pairs(region, blocks, across, within, slots, out, 0)
    landed(in_flight(pairs, sems))


def first_half(rows):
    return iota(rows.shape, 1) < 4


def interleaved(first, second):
    first, second = (rows.reshape(16, 8, 256) for rows in (first, second))
    here = first_half(first)
    even = jnp.where(here, first, pltpu.roll(second, 4, 1))
    odd = jnp.where(here, pltpu.roll(first, 4, 1), second)
    return jnp.stack([even, odd], axis=1).reshape(PEERS, 8, 256)


def separated(rows):
    rows = rows.reshape(16, 2, 8, 256)
    even, odd = rows[:, 0], rows[:, 1]
    here = first_half(even)
    first = jnp.where(here, even, pltpu.roll(odd, 4, 1))
    second = jnp.where(here, pltpu.roll(even, 4, 1), odd)
    return first.reshape(128, 256), second.reshape(128, 256)


def grams_of(me, region, lists, val, wgt, across, within, gathered, group):
    lane = iota((128, 128), 1)
    row = iota((128, 128), 0) & 3
    top, low = [], []
    for half in range(2):
        slot = 2 * me[0] + half
        own = jnp.minimum(slot, HOME - 1)
        slot = jnp.maximum(slot - HOME, 0)
        from_right = jnp.where(slot < HANDED, 1, 0)
        place = HANDED + (slot & (HANDED - 1))
        handed = jnp.where(
            (region[0] & 1) == from_right,
            across[place].astype(F32),
            within[place].astype(F32),
        )
        is_own = 2 * me[0] + half < HOME
        w = jnp.where(is_own, wide_row(wgt[own]), handed[0:1] + handed[1:2])
        v = jnp.where(is_own, wide_row(val[own]), handed[2:3] + handed[3:4])
        y = gathered[:, group + half].astype(F32).reshape(MEMBERS, OBS)
        scaled = (y * w).astype(BF16)
        gram = lax.dot_general(
            y.astype(BF16), scaled, (((1,), (1,)), ((), ())), preferred_element_type=F32
        )
        vector = jnp.sum(y * (w * v), axis=1, keepdims=True)
        vector_high = rounded(vector)
        vector_low = vector - vector_high
        coeff = lists[8 * half : 8 * half + 1]
        coeff_high = rounded(coeff)
        extra = jnp.where(row == 0, coeff_high, jnp.where(row == 1, coeff - coeff_high, 0.0))
        for place, column in enumerate(
            (vector_high[:128], vector_low[:128], vector_high[128:], vector_low[128:])
        ):
            extra = jnp.where(lane == place, column, extra)
        top.append(gram[:128, :])
        low.append(jnp.concatenate([gram[128:, 128:], extra], axis=1))
    return interleaved(*top).astype(BF16), interleaved(*low).astype(BF16)


def gram_kernel(*refs):
    *about, gathered, out = refs
    out[:, 0], out[:, 1] = grams_of(*about, gathered, gathered.shape[1] - 2)


def pick_kernel(region, chosen, blocks, val, wgt, across, within, held, vals, wgts, sems):
    odd = region[0] & 1
    sides = ((1 - odd, across), (odd, within))
    landed(in_flight([(blocks, held), (val, vals), (wgt, wgts)], sems))
    row = iota((OWN, OBS), 0)
    for side, out in sides:
        for k in range(HANDED):
            block = chosen[side, k]
            out[k] = held[block]
            w, v = wide_row(wgts[block]), wide_row(vals[block])
            w_high, v_high = rounded(w), rounded(v)
            tail = jnp.where(row == 2, v_high, jnp.where(row == 3, v - v_high, 0.0))
            tail = jnp.where(row == 0, w_high, jnp.where(row == 1, w - w_high, tail))
            out[HANDED + k] = tail.astype(BF16)


def lists_kernel(table, damping, tally, out):
    slot_of_lane = iota((1, 128), 1) - 64
    for half in range(2):
        coeff = jnp.zeros((1, 128), F32)
        for position in range(MAXL):
            used = jnp.where(position < tally[half], damping[half, position], 0.0)
            slot = (table[half, position] - HANDED) & (EXT - 1)
            coeff = coeff + jnp.where(slot_of_lane == slot, used, 0.0)
        out[half * 8 : (half + 1) * 8] = jnp.broadcast_to(coeff, (8, 128))


def sums_of(x):
    coeffs = x[:, 1, :, 128:]
    here = first_half(coeffs)
    high = jnp.where(here, coeffs[:, 0:1], coeffs[:, 4:5]).reshape(256, 128)
    low = jnp.where(here, coeffs[:, 1:2], coeffs[:, 5:6]).reshape(256, 128)
    spread_out = one_hot_lanes((128, 256))
    wide = dot(jnp.concatenate([high, low], axis=0).astype(BF16), spread_out)
    same = ((iota((256, 256), 0) ^ iota((256, 256), 1)) & 3) == 0
    high = jnp.where(same, wide[:256], 0.0).astype(BF16)
    low = jnp.where(same, wide[256:], 0.0).astype(BF16)
    total = []
    for part in range(2):
        rows = x[:, part].reshape(256, 256).astype(BF16)
        total.append(dot(high, rows) + dot(low, rows))
    tail = total[1][:, 128:]
    both = tail + pltpu.roll(tail, 127, 1)
    high = rounded(both)
    low = pltpu.roll(both - high, 1, 1)
    lane = iota((256, 128), 1)
    tail = jnp.where(lane < 4, jnp.where((lane & 1) == 0, high, low), tail)
    tail = jnp.concatenate([total[1][:, :128], tail], axis=1)
    return (rows.reshape(PEERS, 8, 256).astype(BF16) for rows in (total[0], tail))


def combine_kernel(entries, fields, out, pert, centre):
    centre_kernel(fields, pert, centre)
    out[:, 0], out[:, 1] = sums_of(entries[...].astype(F32))


def combine_and_pack_kernel(entries, fields, out, part, sems):
    copies = in_flight(field_pairs(fields, out), sems)
    part[:, 0], part[:, 1] = sums_of(entries[...].astype(F32))
    last = pltpu.make_async_copy(part, out.at[:, pl.ds(LEVELS, 2)], sems.at[LEVELS])
    last.start()
    landed(copies)
    last.wait()


def centre_kernel(fields, pert, centre, entries=None):
    if entries is not None:
        entries[...] = fields[:, LEVELS:]
    for level in range(LEVELS):
        x = fields[:, level].astype(F32).reshape(MEMBERS, COLS)
        mean = jnp.sum(x, axis=0, keepdims=True) / MEMBERS
        away = (x - mean).astype(BF16)
        for half in range(2):
            at = slice(level * 128, (level + 1) * 128)
            pert[half, :, at] = away[:, half * 128 : (half + 1) * 128]
            centre[half, :, at] = jnp.broadcast_to(
                mean[:, half * 128 : (half + 1) * 128], (8, 128)
            )


def mix_kernel(entries, pert, centre, out):
    x = entries[...].astype(F32)
    tops, lows = separated(x[:, 0]), separated(x[:, 1])
    eye = jnp.where(iota((256, 256), 0) == iota((256, 256), 1), 1.0, 0.0)
    vectors, bounds, a1 = [], [], []
    for half in range(2):
        top, low = tops[half], lows[half]
        gram = jnp.concatenate(
            [top, jnp.concatenate([top[:, 128:].T, low[:, :128]], axis=1)], axis=0
        )
        vectors.append(
            jnp.concatenate(
                [low[:, 128:129] + low[:, 129:130], low[:, 130:131] + low[:, 131:132]], axis=0
            )
        )
        system = eye + gram * (1.0 / (MEMBERS - 1.0))
        sums = jnp.sum(jnp.abs(system), axis=1, keepdims=True)
        bound = jnp.max(sums, axis=0, keepdims=True)
        bounds.append(bound)
        a1.append(system / bound)
    s1 = [split(a) for a in a1]
    a2 = [single(a, a) for a in a1]
    a3 = [single(a, b) for a, b in zip(a2, a1)]
    a4 = [single(a, a) for a in a2]
    z2 = [
        2.25 * eye - 2.4375 * a + 1.6875 * b - 0.5625 * c + 0.0625 * d
        for a, b, c, d in zip(a1, a2, a3, a4)
    ]
    t2 = [split(z) for z in z2]
    az = [split(product(s, t)) for s, t in zip(s1, t2)]
    zz = [split(product(t, t)) for t in t2]
    z3 = [1.5 * z - 0.5 * product(a, b) for z, a, b in zip(z2, az, zz)]
    for half in range(2):
        spread = z3[half] / jnp.sqrt(bounds[half])
        across = jnp.sum(eye * vectors[half], axis=0, keepdims=True)
        inner = jnp.sum(spread * across, axis=1, keepdims=True)
        shift = jnp.sum(spread * inner, axis=0, keepdims=True) / (MEMBERS - 1.0)
        mixing = (spread + shift).astype(BF16)
        result = dot(mixing, pert[half]) + centre[half][:1]
        for level in range(LEVELS):
            rows = result[:, level * 128 : (level + 1) * 128].reshape(PEERS, OWN, 128)
            out[:, level, :, half * 128 : (half + 1) * 128] = rows.astype(BF16)


def unpack_kernel(parts, out, sems):
    landed(in_flight([(parts.at[:, level], out.at[level]) for level in range(LEVELS)], sems))


def swapped(value, first):
    pairs = []
    for i in range(first, lax.axis_size("region") - 1, 2):
        pairs += [(i, i + 1), (i + 1, i)]
    return lax.ppermute(value, "region", pairs)


def exchange(value):
    return lax.all_to_all(value, "member", split_axis=0, concat_axis=0, tiled=True)


def shape(*dims, dtype=BF16):
    return jax.ShapeDtypeStruct(dims, dtype)


CENTRED = (shape(2, MEMBERS, LEVELS * 128), shape(2, 8, LEVELS * 128, dtype=F32))


WITH_FIELDS = [pltpu.VMEM((PEERS, 2, 8, 256), BF16), pltpu.SemaphoreType.DMA((LEVELS + 1,))]


def on_device(
    background_trajectories,
    sensor_spread_matrix,
    departure_vector,
    inverse_error_variance,
    edge_tile_handoff,
    measurement_tile_table,
    distance_damping,
    active_tile_tally,
):
    val = departure_vector.reshape(HOME, 2, 128)
    wgt = inverse_error_variance.reshape(HOME, 2, 128)
    fields = background_trajectories.reshape(OWN, LEVELS, PEERS, COLS).transpose(1, 2, 0, 3)
    blocks = sensor_spread_matrix.reshape(OWN, HOME, OBS).transpose(1, 0, 2)
    me = lax.axis_index("member").reshape(1)

    region = lax.axis_index("region").reshape(1)
    lists = pl.pallas_call(
        lists_kernel,
        out_shape=shape(16, 128, dtype=F32),
        in_specs=[SCALARS] * 3,
        out_specs=WHOLE,
        compiler_params=PARAMS,
        name="lists",
    )(measurement_tile_table, distance_damping, active_tile_tally)

    across, within = pl.pallas_call(
        pick_kernel,
        out_shape=(shape(2 * HANDED, OWN, OBS),) * 2,
        in_specs=[SCALARS, SCALARS, HBM, HBM, HBM],
        out_specs=(WHOLE, WHOLE),
        scratch_shapes=[
            pltpu.VMEM((HOME, OWN, OBS), BF16),
            pltpu.VMEM((HOME, 2, 128), F32),
            pltpu.VMEM((HOME, 2, 128), F32),
            pltpu.SemaphoreType.DMA((3,)),
        ],
        compiler_params=PARAMS,
        name="pick",
    )(region, edge_tile_handoff, blocks, val, wgt)
    across = swapped(across, 1)
    within = swapped(within, 0)

    def gram(gathered, *about):
        return pl.pallas_call(
            gram_kernel,
            out_shape=shape(PEERS, 2, 8, 256),
            in_specs=[SCALARS] * 2 + [WHOLE] * 6,
            out_specs=WHOLE,
            compiler_params=PARAMS,
            name="gram",
        )(*about, gathered)

    def fields_first(fields, blocks, *about):
        _, region, *_, across, within = about
        packed = pl.pallas_call(
            pack_both_kernel,
            out_shape=shape(PEERS, LEVELS + 2, OWN, COLS),
            in_specs=[SCALARS, HBM, HBM, WHOLE, WHOLE],
            out_specs=ANY,
            scratch_shapes=[
                pltpu.VMEM((HANDED, 2, OWN, COLS), BF16),
                pltpu.SemaphoreType.DMA((2,)),
                pltpu.SemaphoreType.DMA((LEVELS,)),
            ],
            compiler_params=PARAMS,
            name="pack_both",
        )(region, fields, blocks, across, within)
        gathered = exchange(packed)
        grams = exchange(gram(gathered, *about))
        sums, pert, centre = pl.pallas_call(
            combine_kernel,
            out_shape=(shape(PEERS, 2, 8, 256),) + CENTRED,
            in_specs=[WHOLE] * 2,
            out_specs=(WHOLE,) * 3,
            compiler_params=PARAMS,
            name="combine",
        )(grams, gathered)
        return pert, centre, exchange(sums)

    def fields_last(fields, blocks, *about):
        _, region, *_, across, within = about
        packed = pl.pallas_call(
            pack_blocks_kernel,
            out_shape=shape(PEERS, 2, OWN, COLS),
            in_specs=[SCALARS, HBM, WHOLE, WHOLE],
            out_specs=ANY,
            scratch_shapes=[
                pltpu.VMEM((HANDED, 2, OWN, COLS), BF16),
                pltpu.SemaphoreType.DMA((2,)),
            ],
            compiler_params=PARAMS,
            name="pack_blocks",
        )(region, blocks, across, within)
        grams = exchange(gram(exchange(packed), *about))
        sums = pl.pallas_call(
            combine_and_pack_kernel,
            out_shape=shape(PEERS, LEVELS + 2, OWN, COLS),
            in_specs=[WHOLE, HBM],
            out_specs=ANY,
            scratch_shapes=WITH_FIELDS,
            compiler_params=PARAMS,
            name="combine_and_pack",
        )(grams, fields)
        return pl.pallas_call(
            centre_kernel,
            out_shape=CENTRED + (shape(PEERS, 2, 8, 256),),
            in_specs=[WHOLE],
            out_specs=(WHOLE,) * 3,
            compiler_params=PARAMS,
            name="centre_and_part",
        )(exchange(sums))

    even = lax.axis_index("region") % 2 == 0
    about = (me, region, lists, val, wgt, across, within)
    pert, centre, systems = lax.cond(
        even,
        fields_first,
        fields_last,
        fields,
        blocks.reshape(HOME // 2, 2, OWN, OBS),
        *about,
    )

    mixed = pl.pallas_call(
        mix_kernel,
        out_shape=shape(PEERS, LEVELS, OWN, COLS),
        in_specs=[WHOLE] * 3,
        out_specs=WHOLE,
        compiler_params=PARAMS,
        name="mix",
    )(systems, pert, centre)
    analysis = pl.pallas_call(
        unpack_kernel,
        out_shape=shape(LEVELS, PEERS, OWN, COLS),
        in_specs=[ANY],
        out_specs=HBM,
        scratch_shapes=[pltpu.SemaphoreType.DMA((LEVELS,))],
        compiler_params=PARAMS,
        name="unpack",
    )(exchange(mixed))
    return analysis.transpose(2, 0, 1, 3).reshape(OWN, LEVELS, PEERS * COLS)


def solution(mesh):
    placed = (
        P("member", None, "region"),
        P("member", "region"),
        P("region"),
        P("region"),
        P(None, "region"),
        P(("region", "member"), None),
        P(("region", "member"), None),
        P(("region", "member")),
    )
    return jax.shard_map(
        on_device,
        mesh=mesh,
        in_specs=placed,
        out_specs=P("member", None, "region"),
        check_vma=False,
    )
```

```python
import jax
import jax.numpy as jnp
from jax import lax
from jax.experimental import pallas as pl
from jax.experimental.pallas import tpu as pltpu
from jax.sharding import PartitionSpec as P

F32 = jnp.float32
BF16 = jnp.bfloat16
MEMBERS = 256
PEERS = 32
OWN = 8
LEVELS = 6
OBS = 256
HANDED = 4
HOME = 56
EXT = 64
COLS = 256
MAXL = 16
VMEM_BYTES = 48 * 1024 * 1024
WHOLE = pl.BlockSpec(memory_space=pltpu.VMEM)
ANY = pl.BlockSpec(memory_space=pl.ANY)
HBM = pl.BlockSpec(memory_space=pltpu.HBM)
SCALARS = pl.BlockSpec(memory_space=pltpu.SMEM)
PARAMS = pltpu.CompilerParams(vmem_limit_bytes=VMEM_BYTES)


def iota(shape, dim):
    return lax.broadcasted_iota(jnp.int32, shape, dim)


def one_hot_lanes(shape):
    hit = iota(shape, 0) - 64 == (iota(shape, 1) >> 2)
    return jnp.where(hit, 1.0, 0.0).astype(BF16)


def dot(a, b):
    return jnp.dot(a, b, preferred_element_type=F32)


def split(a):
    high = a.astype(BF16)
    return high, (a - high.astype(F32)).astype(BF16)


def single(a, b):
    return dot(a.astype(BF16), b.astype(BF16))


def product(a, b):
    left = jnp.concatenate([a[0], a[0], a[1]], axis=1)
    return dot(left, jnp.concatenate([b[0], b[1], b[0]], axis=0))


def rounded(a):
    return a.astype(BF16).astype(F32)


def in_flight(pairs, sems):
    copies = [pltpu.make_async_copy(*ends, sems.at[k]) for k, ends in enumerate(pairs)]
    for copy in copies:
        copy.start()
    return copies


def landed(copies):
    for copy in copies:
        copy.wait()


def wide_row(pair):
    return jnp.concatenate([pair[:1], pair[1:]], axis=1)


def block_pairs(region, blocks, across, within, slots, out, group):
    odd = (region[0] & 1) == 1
    across = across[:HANDED].astype(F32)
    within = within[:HANDED].astype(F32)
    right = jnp.where(odd, across, within).astype(BF16)
    left = jnp.where(odd, within, across).astype(BF16)
    slots[: HANDED // 2] = right.reshape(HANDED // 2, 2, OWN, OBS)
    slots[HANDED // 2 :] = left.reshape(HANDED // 2, 2, OWN, OBS)
    return [
        (blocks, out.at[pl.ds(0, HOME // 2), pl.ds(group, 2)]),
        (slots, out.at[pl.ds(HOME // 2, HANDED), pl.ds(group, 2)]),
    ]


def field_pairs(fields, out):
    return [(fields.at[level], out.at[:, level]) for level in range(LEVELS)]


def pack_both_kernel(region, fields, blocks, across, within, out, slots, sems, field_sems):
    first = in_flight(field_pairs(fields, out), field_sems)
    pairs = block_pairs(region, blocks, across, within, slots, out, LEVELS)
    landed(first + in_flight(pairs, sems))


def pack_blocks_kernel(region, blocks, across, within, out, slots, sems):
    pairs = block_pairs(region, blocks, across, within, slots, out, 0)
    landed(in_flight(pairs, sems))


def first_half(rows):
    return iota(rows.shape, 1) < 4


def interleaved(first, second):
    first, second = (rows.reshape(16, 8, 256) for rows in (first, second))
    here = first_half(first)
    even = jnp.where(here, first, pltpu.roll(second, 4, 1))
    odd = jnp.where(here, pltpu.roll(first, 4, 1), second)
    return jnp.stack([even, odd], axis=1).reshape(PEERS, 8, 256)


def separated(rows):
    rows = rows.reshape(16, 2, 8, 256)
    even, odd = rows[:, 0], rows[:, 1]
    here = first_half(even)
    first = jnp.where(here, even, pltpu.roll(odd, 4, 1))
    second = jnp.where(here, pltpu.roll(even, 4, 1), odd)
    return first.reshape(128, 256), second.reshape(128, 256)


def grams_of(me, region, lists, val, wgt, across, within, gathered, group):
    lane = iota((128, 128), 1)
    row = iota((128, 128), 0) & 3
    top, low = [], []
    for half in range(2):
        slot = 2 * me[0] + half
        own = jnp.minimum(slot, HOME - 1)
        slot = jnp.maximum(slot - HOME, 0)
        from_right = jnp.where(slot < HANDED, 1, 0)
        place = HANDED + (slot & (HANDED - 1))
        handed = jnp.where(
            (region[0] & 1) == from_right,
            across[place].astype(F32),
            within[place].astype(F32),
        )
        is_own = 2 * me[0] + half < HOME
        w = jnp.where(is_own, wide_row(wgt[own]), handed[0:1] + handed[1:2])
        v = jnp.where(is_own, wide_row(val[own]), handed[2:3] + handed[3:4])
        y = gathered[:, group + half].astype(F32).reshape(MEMBERS, OBS)
        scaled = (y * w).astype(BF16)
        gram = lax.dot_general(
            y.astype(BF16), scaled, (((1,), (1,)), ((), ())), preferred_element_type=F32
        )
        vector = jnp.sum(y * (w * v), axis=1, keepdims=True)
        vector_high = rounded(vector)
        vector_low = vector - vector_high
        coeff = lists[8 * half : 8 * half + 1]
        coeff_high = rounded(coeff)
        extra = jnp.where(row == 0, coeff_high, jnp.where(row == 1, coeff - coeff_high, 0.0))
        for place, column in enumerate(
            (vector_high[:128], vector_low[:128], vector_high[128:], vector_low[128:])
        ):
            extra = jnp.where(lane == place, column, extra)
        top.append(gram[:128, :])
        low.append(jnp.concatenate([gram[128:, 128:], extra], axis=1))
    return interleaved(*top).astype(BF16), interleaved(*low).astype(BF16)


def gram_kernel(*refs):
    *about, gathered, out = refs
    out[:, 0], out[:, 1] = grams_of(*about, gathered, gathered.shape[1] - 2)


def pick_kernel(region, chosen, blocks, val, wgt, across, within, held, vals, wgts, sems):
    odd = region[0] & 1
    sides = ((1 - odd, across), (odd, within))
    landed(in_flight([(blocks, held), (val, vals), (wgt, wgts)], sems))
    row = iota((OWN, OBS), 0)
    for side, out in sides:
        for k in range(HANDED):
            block = chosen[side, k]
            out[k] = held[block]
            w, v = wide_row(wgts[block]), wide_row(vals[block])
            w_high, v_high = rounded(w), rounded(v)
            tail = jnp.where(row == 2, v_high, jnp.where(row == 3, v - v_high, 0.0))
            tail = jnp.where(row == 0, w_high, jnp.where(row == 1, w - w_high, tail))
            out[HANDED + k] = tail.astype(BF16)


def lists_kernel(table, damping, tally, out):
    slot_of_lane = iota((1, 128), 1) - 64
    for half in range(2):
        coeff = jnp.zeros((1, 128), F32)
        for position in range(MAXL):
            used = jnp.where(position < tally[half], damping[half, position], 0.0)
            slot = (table[half, position] - HANDED) & (EXT - 1)
            coeff = coeff + jnp.where(slot_of_lane == slot, used, 0.0)
        out[half * 8 : (half + 1) * 8] = jnp.broadcast_to(coeff, (8, 128))


def sums_of(x):
    coeffs = x[:, 1, :, 128:]
    here = first_half(coeffs)
    high = jnp.where(here, coeffs[:, 0:1], coeffs[:, 4:5]).reshape(256, 128)
    low = jnp.where(here, coeffs[:, 1:2], coeffs[:, 5:6]).reshape(256, 128)
    spread_out = one_hot_lanes((128, 256))
    wide = dot(jnp.concatenate([high, low], axis=0).astype(BF16), spread_out)
    same = ((iota((256, 256), 0) ^ iota((256, 256), 1)) & 3) == 0
    high = jnp.where(same, wide[:256], 0.0).astype(BF16)
    low = jnp.where(same, wide[256:], 0.0).astype(BF16)
    total = []
    for part in range(2):
        rows = x[:, part].reshape(256, 256).astype(BF16)
        total.append(dot(high, rows) + dot(low, rows))
    tail = total[1][:, 128:]
    both = tail + pltpu.roll(tail, 127, 1)
    high = rounded(both)
    low = pltpu.roll(both - high, 1, 1)
    lane = iota((256, 128), 1)
    tail = jnp.where(lane < 4, jnp.where((lane & 1) == 0, high, low), tail)
    tail = jnp.concatenate([total[1][:, :128], tail], axis=1)
    return (rows.reshape(PEERS, 8, 256).astype(BF16) for rows in (total[0], tail))


def combine_kernel(entries, fields, out, pert, centre):
    centre_kernel(fields, pert, centre)
    out[:, 0], out[:, 1] = sums_of(entries[...].astype(F32))


def combine_and_pack_kernel(entries, fields, out, part, sems):
    copies = in_flight(field_pairs(fields, out), sems)
    part[:, 0], part[:, 1] = sums_of(entries[...].astype(F32))
    last = pltpu.make_async_copy(part, out.at[:, pl.ds(LEVELS, 2)], sems.at[LEVELS])
    last.start()
    landed(copies)
    last.wait()


def centre_kernel(fields, pert, centre, entries=None):
    if entries is not None:
        entries[...] = fields[:, LEVELS:]
    for level in range(LEVELS):
        x = fields[:, level].astype(F32).reshape(MEMBERS, COLS)
        mean = jnp.sum(x, axis=0, keepdims=True) / MEMBERS
        away = (x - mean).astype(BF16)
        for half in range(2):
            at = slice(level * 128, (level + 1) * 128)
            pert[half, :, at] = away[:, half * 128 : (half + 1) * 128]
            centre[half, :, at] = jnp.broadcast_to(
                mean[:, half * 128 : (half + 1) * 128], (8, 128)
            )


def mix_kernel(entries, pert, centre, out):
    x = entries[...].astype(F32)
    tops, lows = separated(x[:, 0]), separated(x[:, 1])
    eye = jnp.where(iota((256, 256), 0) == iota((256, 256), 1), 1.0, 0.0)
    vectors, bounds, a1 = [], [], []
    for half in range(2):
        top, low = tops[half], lows[half]
        gram = jnp.concatenate(
            [top, jnp.concatenate([top[:, 128:].T, low[:, :128]], axis=1)], axis=0
        )
        vectors.append(
            jnp.concatenate(
                [low[:, 128:129] + low[:, 129:130], low[:, 130:131] + low[:, 131:132]], axis=0
            )
        )
        system = eye + gram * (1.0 / (MEMBERS - 1.0))
        sums = jnp.sum(jnp.abs(system), axis=1, keepdims=True)
        bound = jnp.max(sums, axis=0, keepdims=True)
        bounds.append(bound)
        a1.append(system / bound)
    a2 = [single(a, a) for a in a1]
    a3 = [single(a, b) for a, b in zip(a2, a1)]
    a4 = [single(a, a) for a in a2]
    w = [
        2.4375 * a - 1.6875 * b + 0.5625 * c - 0.0625 * d
        for a, b, c, d in zip(a1, a2, a3, a4)
    ]
    z2 = [2.25 * eye - d for d in w]
    az = [split(2.25 * a - single(a, d)) for a, d in zip(a1, w)]
    zz = [split(5.0625 * eye - 4.5 * d + single(d, d)) for d in w]
    z3 = [1.5 * z - 0.5 * product(a, b) for z, a, b in zip(z2, az, zz)]
    for half in range(2):
        spread = z3[half] / jnp.sqrt(bounds[half])
        across = jnp.sum(eye * vectors[half], axis=0, keepdims=True)
        inner = jnp.sum(spread * across, axis=1, keepdims=True)
        shift = jnp.sum(spread * inner, axis=0, keepdims=True) / (MEMBERS - 1.0)
        mixing = (spread + shift).astype(BF16)
        result = dot(mixing, pert[half]) + centre[half][:1]
        for level in range(LEVELS):
            rows = result[:, level * 128 : (level + 1) * 128].reshape(PEERS, OWN, 128)
            out[:, level, :, half * 128 : (half + 1) * 128] = rows.astype(BF16)


def unpack_kernel(parts, out, sems):
    landed(in_flight([(parts.at[:, level], out.at[level]) for level in range(LEVELS)], sems))


def swapped(value, first):
    pairs = []
    for i in range(first, lax.axis_size("region") - 1, 2):
        pairs += [(i, i + 1), (i + 1, i)]
    return lax.ppermute(value, "region", pairs)


def exchange(value):
    return lax.all_to_all(value, "member", split_axis=0, concat_axis=0, tiled=True)


def shape(*dims, dtype=BF16):
    return jax.ShapeDtypeStruct(dims, dtype)


CENTRED = (shape(2, MEMBERS, LEVELS * 128), shape(2, 8, LEVELS * 128, dtype=F32))


WITH_FIELDS = [pltpu.VMEM((PEERS, 2, 8, 256), BF16), pltpu.SemaphoreType.DMA((LEVELS + 1,))]


def on_device(
    background_trajectories,
    sensor_spread_matrix,
    departure_vector,
    inverse_error_variance,
    edge_tile_handoff,
    measurement_tile_table,
    distance_damping,
    active_tile_tally,
):
    val = departure_vector.reshape(HOME, 2, 128)
    wgt = inverse_error_variance.reshape(HOME, 2, 128)
    fields = background_trajectories.reshape(OWN, LEVELS, PEERS, COLS).transpose(1, 2, 0, 3)
    blocks = sensor_spread_matrix.reshape(OWN, HOME, OBS).transpose(1, 0, 2)
    me = lax.axis_index("member").reshape(1)

    region = lax.axis_index("region").reshape(1)
    lists = pl.pallas_call(
        lists_kernel,
        out_shape=shape(16, 128, dtype=F32),
        in_specs=[SCALARS] * 3,
        out_specs=WHOLE,
        compiler_params=PARAMS,
        name="lists",
    )(measurement_tile_table, distance_damping, active_tile_tally)

    across, within = pl.pallas_call(
        pick_kernel,
        out_shape=(shape(2 * HANDED, OWN, OBS),) * 2,
        in_specs=[SCALARS, SCALARS, HBM, HBM, HBM],
        out_specs=(WHOLE, WHOLE),
        scratch_shapes=[
            pltpu.VMEM((HOME, OWN, OBS), BF16),
            pltpu.VMEM((HOME, 2, 128), F32),
            pltpu.VMEM((HOME, 2, 128), F32),
            pltpu.SemaphoreType.DMA((3,)),
        ],
        compiler_params=PARAMS,
        name="pick",
    )(region, edge_tile_handoff, blocks, val, wgt)
    across = swapped(across, 1)
    within = swapped(within, 0)

    def gram(gathered, *about):
        return pl.pallas_call(
            gram_kernel,
            out_shape=shape(PEERS, 2, 8, 256),
            in_specs=[SCALARS] * 2 + [WHOLE] * 6,
            out_specs=WHOLE,
            compiler_params=PARAMS,
            name="gram",
        )(*about, gathered)

    def fields_first(fields, blocks, *about):
        _, region, *_, across, within = about
        packed = pl.pallas_call(
            pack_both_kernel,
            out_shape=shape(PEERS, LEVELS + 2, OWN, COLS),
            in_specs=[SCALARS, HBM, HBM, WHOLE, WHOLE],
            out_specs=ANY,
            scratch_shapes=[
                pltpu.VMEM((HANDED, 2, OWN, COLS), BF16),
                pltpu.SemaphoreType.DMA((2,)),
                pltpu.SemaphoreType.DMA((LEVELS,)),
            ],
            compiler_params=PARAMS,
            name="pack_both",
        )(region, fields, blocks, across, within)
        gathered = exchange(packed)
        grams = exchange(gram(gathered, *about))
        sums, pert, centre = pl.pallas_call(
            combine_kernel,
            out_shape=(shape(PEERS, 2, 8, 256),) + CENTRED,
            in_specs=[WHOLE] * 2,
            out_specs=(WHOLE,) * 3,
            compiler_params=PARAMS,
            name="combine",
        )(grams, gathered)
        return pert, centre, exchange(sums)

    def fields_last(fields, blocks, *about):
        _, region, *_, across, within = about
        packed = pl.pallas_call(
            pack_blocks_kernel,
            out_shape=shape(PEERS, 2, OWN, COLS),
            in_specs=[SCALARS, HBM, WHOLE, WHOLE],
            out_specs=ANY,
            scratch_shapes=[
                pltpu.VMEM((HANDED, 2, OWN, COLS), BF16),
                pltpu.SemaphoreType.DMA((2,)),
            ],
            compiler_params=PARAMS,
            name="pack_blocks",
        )(region, blocks, across, within)
        grams = exchange(gram(exchange(packed), *about))
        sums = pl.pallas_call(
            combine_and_pack_kernel,
            out_shape=shape(PEERS, LEVELS + 2, OWN, COLS),
            in_specs=[WHOLE, HBM],
            out_specs=ANY,
            scratch_shapes=WITH_FIELDS,
            compiler_params=PARAMS,
            name="combine_and_pack",
        )(grams, fields)
        return pl.pallas_call(
            centre_kernel,
            out_shape=CENTRED + (shape(PEERS, 2, 8, 256),),
            in_specs=[WHOLE],
            out_specs=(WHOLE,) * 3,
            compiler_params=PARAMS,
            name="centre_and_part",
        )(exchange(sums))

    even = lax.axis_index("region") % 2 == 0
    about = (me, region, lists, val, wgt, across, within)
    pert, centre, systems = lax.cond(
        even,
        fields_first,
        fields_last,
        fields,
        blocks.reshape(HOME // 2, 2, OWN, OBS),
        *about,
    )

    mixed = pl.pallas_call(
        mix_kernel,
        out_shape=shape(PEERS, LEVELS, OWN, COLS),
        in_specs=[WHOLE] * 3,
        out_specs=WHOLE,
        compiler_params=PARAMS,
        name="mix",
    )(systems, pert, centre)
    analysis = pl.pallas_call(
        unpack_kernel,
        out_shape=shape(LEVELS, PEERS, OWN, COLS),
        in_specs=[ANY],
        out_specs=HBM,
        scratch_shapes=[pltpu.SemaphoreType.DMA((LEVELS,))],
        compiler_params=PARAMS,
        name="unpack",
    )(exchange(mixed))
    return analysis.transpose(2, 0, 1, 3).reshape(OWN, LEVELS, PEERS * COLS)


def solution(mesh):
    placed = (
        P("member", None, "region"),
        P("member", "region"),
        P("region"),
        P("region"),
        P(None, "region"),
        P(("region", "member"), None),
        P(("region", "member"), None),
        P(("region", "member")),
    )
    return jax.shard_map(
        on_device,
        mesh=mesh,
        in_specs=placed,
        out_specs=P("member", None, "region"),
        check_vma=False,
    )
```

```python
import functools

import jax
import jax.numpy as jnp
from jax import lax
from jax.experimental import pallas as pl
from jax.experimental.pallas import tpu as pltpu
from jax.sharding import PartitionSpec as P

F32 = jnp.float32
BF16 = jnp.bfloat16
MEMBERS = 256
PEERS = 32
OWN = 8
LEVELS = 6
OBS = 256
HANDED = 4
HOME = 56
EXT = 64
COLS = 256
MAXL = 16
VMEM_BYTES = 48 * 1024 * 1024
WHOLE = pl.BlockSpec(memory_space=pltpu.VMEM)
ANY = pl.BlockSpec(memory_space=pl.ANY)
HBM = pl.BlockSpec(memory_space=pltpu.HBM)
SCALARS = pl.BlockSpec(memory_space=pltpu.SMEM)
EVEN = (5, 1, 0)
ODD = (0, 0, 6)
PARAMS = pltpu.CompilerParams(vmem_limit_bytes=VMEM_BYTES)


def iota(shape, dim):
    return lax.broadcasted_iota(jnp.int32, shape, dim)


def one_hot_lanes(shape):
    hit = iota(shape, 0) - 64 == (iota(shape, 1) >> 2)
    return jnp.where(hit, 1.0, 0.0).astype(BF16)


def dot(a, b):
    return jnp.dot(a, b, preferred_element_type=F32)


def split(a):
    high = a.astype(BF16)
    return high, (a - high.astype(F32)).astype(BF16)


def single(a, b):
    return dot(a.astype(BF16), b.astype(BF16))


def product(a, b):
    left = jnp.concatenate([a[0], a[0], a[1]], axis=1)
    return dot(left, jnp.concatenate([b[0], b[1], b[0]], axis=0))


def rounded(a):
    return a.astype(BF16).astype(F32)


def in_flight(pairs, sems):
    copies = [pltpu.make_async_copy(*ends, sems.at[k]) for k, ends in enumerate(pairs)]
    for copy in copies:
        copy.start()
    return copies


def landed(copies):
    for copy in copies:
        copy.wait()


def wide_row(pair):
    return jnp.concatenate([pair[:1], pair[1:]], axis=1)


def block_pairs(region, blocks, across, within, slots, out, group):
    odd = (region[0] & 1) == 1
    across = across[:HANDED].astype(F32)
    within = within[:HANDED].astype(F32)
    right = jnp.where(odd, across, within).astype(BF16)
    left = jnp.where(odd, within, across).astype(BF16)
    slots[: HANDED // 2] = right.reshape(HANDED // 2, 2, OWN, OBS)
    slots[HANDED // 2 :] = left.reshape(HANDED // 2, 2, OWN, OBS)
    return [
        (blocks, out.at[pl.ds(0, HOME // 2), pl.ds(group, 2)]),
        (slots, out.at[pl.ds(HOME // 2, HANDED), pl.ds(group, 2)]),
    ]


def field_pairs(fields, out, levels):
    return [(fields.at[level], out.at[:, place]) for place, level in enumerate(levels)]


def pack_kernel(levels, region, fields, blocks, across, within, out, slots, sems):
    first = in_flight(field_pairs(fields, out, levels), sems)
    pairs = block_pairs(region, blocks, across, within, slots, out, len(levels))
    last = [
        pltpu.make_async_copy(*ends, sems.at[LEVELS + k]) for k, ends in enumerate(pairs)
    ]
    for copy in last:
        copy.start()
    landed(first + last)


def emit(levels, parts, fields, out, part, sems):
    if not levels:
        out[:, 0], out[:, 1] = parts()
        return
    copies = in_flight(field_pairs(fields, out, levels), sems)
    part[:, 0], part[:, 1] = parts()
    last = pltpu.make_async_copy(part, out.at[:, pl.ds(len(levels), 2)], sems.at[LEVELS])
    last.start()
    landed(copies + [last])


def first_half(rows):
    return iota(rows.shape, 1) < 4


def interleaved(first, second):
    first, second = (rows.reshape(16, 8, 256) for rows in (first, second))
    here = first_half(first)
    even = jnp.where(here, first, pltpu.roll(second, 4, 1))
    odd = jnp.where(here, pltpu.roll(first, 4, 1), second)
    return jnp.stack([even, odd], axis=1).reshape(PEERS, 8, 256)


def separated(rows):
    rows = rows.reshape(16, 2, 8, 256)
    even, odd = rows[:, 0], rows[:, 1]
    here = first_half(even)
    first = jnp.where(here, even, pltpu.roll(odd, 4, 1))
    second = jnp.where(here, pltpu.roll(even, 4, 1), odd)
    return first.reshape(128, 256), second.reshape(128, 256)


def grams_of(me, region, lists, val, wgt, across, within, gathered, group):
    lane = iota((128, 128), 1)
    row = iota((128, 128), 0) & 3
    top, low = [], []
    for half in range(2):
        slot = 2 * me[0] + half
        own = jnp.minimum(slot, HOME - 1)
        slot = jnp.maximum(slot - HOME, 0)
        from_right = jnp.where(slot < HANDED, 1, 0)
        place = HANDED + (slot & (HANDED - 1))
        handed = jnp.where(
            (region[0] & 1) == from_right,
            across[place].astype(F32),
            within[place].astype(F32),
        )
        is_own = 2 * me[0] + half < HOME
        w = jnp.where(is_own, wide_row(wgt[own]), handed[0:1] + handed[1:2])
        v = jnp.where(is_own, wide_row(val[own]), handed[2:3] + handed[3:4])
        y = gathered[:, group + half].astype(F32).reshape(MEMBERS, OBS)
        scaled = (y * w).astype(BF16)
        gram = lax.dot_general(
            y.astype(BF16), scaled, (((1,), (1,)), ((), ())), preferred_element_type=F32
        )
        vector = jnp.sum(y * (w * v), axis=1, keepdims=True)
        vector_high = rounded(vector)
        vector_low = vector - vector_high
        coeff = lists[8 * half : 8 * half + 1]
        coeff_high = rounded(coeff)
        extra = jnp.where(row == 0, coeff_high, jnp.where(row == 1, coeff - coeff_high, 0.0))
        for place, column in enumerate(
            (vector_high[:128], vector_low[:128], vector_high[128:], vector_low[128:])
        ):
            extra = jnp.where(lane == place, column, extra)
        top.append(gram[:128, :])
        low.append(jnp.concatenate([gram[128:, 128:], extra], axis=1))
    return interleaved(*top).astype(BF16), interleaved(*low).astype(BF16)


def gram_kernel(levels, *refs):
    *about, gathered, fields, out, part, sems = refs
    group = gathered.shape[1] - 2
    emit(levels, lambda: grams_of(*about, gathered, group), fields, out, part, sems)


def pick_kernel(region, chosen, blocks, val, wgt, across, within, held, vals, wgts, sems):
    odd = region[0] & 1
    sides = ((1 - odd, across), (odd, within))
    landed(in_flight([(blocks, held), (val, vals), (wgt, wgts)], sems))
    row = iota((OWN, OBS), 0)
    for side, out in sides:
        for k in range(HANDED):
            block = chosen[side, k]
            out[k] = held[block]
            w, v = wide_row(wgts[block]), wide_row(vals[block])
            w_high, v_high = rounded(w), rounded(v)
            tail = jnp.where(row == 2, v_high, jnp.where(row == 3, v - v_high, 0.0))
            tail = jnp.where(row == 0, w_high, jnp.where(row == 1, w - w_high, tail))
            out[HANDED + k] = tail.astype(BF16)


def lists_kernel(table, damping, tally, out):
    slot_of_lane = iota((1, 128), 1) - 64
    for half in range(2):
        coeff = jnp.zeros((1, 128), F32)
        for position in range(MAXL):
            used = jnp.where(position < tally[half], damping[half, position], 0.0)
            slot = (table[half, position] - HANDED) & (EXT - 1)
            coeff = coeff + jnp.where(slot_of_lane == slot, used, 0.0)
        out[half * 8 : (half + 1) * 8] = jnp.broadcast_to(coeff, (8, 128))


def sums_of(x):
    coeffs = x[:, 1, :, 128:]
    here = first_half(coeffs)
    high = jnp.where(here, coeffs[:, 0:1], coeffs[:, 4:5]).reshape(256, 128)
    low = jnp.where(here, coeffs[:, 1:2], coeffs[:, 5:6]).reshape(256, 128)
    spread_out = one_hot_lanes((128, 256))
    wide = dot(jnp.concatenate([high, low], axis=0).astype(BF16), spread_out)
    same = ((iota((256, 256), 0) ^ iota((256, 256), 1)) & 3) == 0
    high = jnp.where(same, wide[:256], 0.0).astype(BF16)
    low = jnp.where(same, wide[256:], 0.0).astype(BF16)
    total = []
    for part in range(2):
        rows = x[:, part].reshape(256, 256).astype(BF16)
        total.append(dot(high, rows) + dot(low, rows))
    tail = total[1][:, 128:]
    both = tail + pltpu.roll(tail, 127, 1)
    high = rounded(both)
    low = pltpu.roll(both - high, 1, 1)
    lane = iota((256, 128), 1)
    tail = jnp.where(lane < 4, jnp.where((lane & 1) == 0, high, low), tail)
    tail = jnp.concatenate([total[1][:, :128], tail], axis=1)
    return (rows.reshape(PEERS, 8, 256).astype(BF16) for rows in (total[0], tail))


def combine_kernel(levels, earlier, entries, fields, *refs):
    if levels:
        out, part, sems = refs
    else:
        *sources, out, pert, centre, part, sems = refs
        centre_of(earlier, [entries if ref is None else ref for ref in sources], pert, centre)
    group = entries.shape[1] - 2
    emit(levels, lambda: sums_of(entries[:, group:].astype(F32)), fields, out, part, sems)


def centre_of(earlier, sources, pert, centre):
    for levels, fields in zip(earlier, sources):
        for place, level in enumerate(levels):
            x = fields[:, place].astype(F32).reshape(MEMBERS, COLS)
            mean = jnp.sum(x, axis=0, keepdims=True) / MEMBERS
            away = (x - mean).astype(BF16)
            for half in range(2):
                at = slice(level * 128, (level + 1) * 128)
                pert[half, :, at] = away[:, half * 128 : (half + 1) * 128]
                centre[half, :, at] = jnp.broadcast_to(
                    mean[:, half * 128 : (half + 1) * 128], (8, 128)
                )


def last_kernel(earlier, *refs):
    *sources, pert, centre, systems = refs
    centre_of(earlier, sources, pert, centre)
    systems[...] = sources[-1][:, len(earlier[-1]) :]


def mix_kernel(entries, pert, centre, out):
    x = entries[...].astype(F32)
    tops, lows = separated(x[:, 0]), separated(x[:, 1])
    eye = jnp.where(iota((256, 256), 0) == iota((256, 256), 1), 1.0, 0.0)
    vectors, bounds, a1 = [], [], []
    for half in range(2):
        top, low = tops[half], lows[half]
        gram = jnp.concatenate(
            [top, jnp.concatenate([top[:, 128:].T, low[:, :128]], axis=1)], axis=0
        )
        vectors.append(
            jnp.concatenate(
                [low[:, 128:129] + low[:, 129:130], low[:, 130:131] + low[:, 131:132]], axis=0
            )
        )
        system = eye + gram * (1.0 / (MEMBERS - 1.0))
        sums = jnp.sum(jnp.abs(system), axis=1, keepdims=True)
        bound = jnp.max(sums, axis=0, keepdims=True)
        bounds.append(bound)
        a1.append(system / bound)
    s1 = [split(a) for a in a1]
    a2 = [single(a, a) for a in a1]
    a3 = [single(a, b) for a, b in zip(a2, a1)]
    a4 = [single(a, a) for a in a2]
    z2 = [
        2.25 * eye - 2.4375 * a + 1.6875 * b - 0.5625 * c + 0.0625 * d
        for a, b, c, d in zip(a1, a2, a3, a4)
    ]
    t2 = [split(z) for z in z2]
    az = [split(product(s, t)) for s, t in zip(s1, t2)]
    zz = [split(product(t, t)) for t in t2]
    z3 = [1.5 * z - 0.5 * product(a, b) for z, a, b in zip(z2, az, zz)]
    for half in range(2):
        spread = z3[half] / jnp.sqrt(bounds[half])
        across = jnp.sum(eye * vectors[half], axis=0, keepdims=True)
        inner = jnp.sum(spread * across, axis=1, keepdims=True)
        shift = jnp.sum(spread * inner, axis=0, keepdims=True) / (MEMBERS - 1.0)
        mixing = (spread + shift).astype(BF16)
        result = dot(mixing, pert[half]) + centre[half][:1]
        for level in range(LEVELS):
            rows = result[:, level * 128 : (level + 1) * 128].reshape(PEERS, OWN, 128)
            out[:, level, :, half * 128 : (half + 1) * 128] = rows.astype(BF16)


def unpack_kernel(parts, out, sems):
    landed(in_flight([(parts.at[:, level], out.at[level]) for level in range(LEVELS)], sems))


def swapped(value, first):
    pairs = []
    for i in range(first, lax.axis_size("region") - 1, 2):
        pairs += [(i, i + 1), (i + 1, i)]
    return lax.ppermute(value, "region", pairs)


def exchange(value):
    return lax.all_to_all(value, "member", split_axis=0, concat_axis=0, tiled=True)


def shape(*dims, dtype=BF16):
    return jax.ShapeDtypeStruct(dims, dtype)


CENTRED = (shape(2, MEMBERS, LEVELS * 128), shape(2, 8, LEVELS * 128, dtype=F32))


def on_device(
    background_trajectories,
    sensor_spread_matrix,
    departure_vector,
    inverse_error_variance,
    edge_tile_handoff,
    measurement_tile_table,
    distance_damping,
    active_tile_tally,
):
    val = departure_vector.reshape(HOME, 2, 128)
    wgt = inverse_error_variance.reshape(HOME, 2, 128)
    fields = background_trajectories.reshape(OWN, LEVELS, PEERS, COLS).transpose(1, 2, 0, 3)
    blocks = sensor_spread_matrix.reshape(OWN, HOME, OBS).transpose(1, 0, 2)
    me = lax.axis_index("member").reshape(1)

    region = lax.axis_index("region").reshape(1)
    lists = pl.pallas_call(
        lists_kernel,
        out_shape=shape(16, 128, dtype=F32),
        in_specs=[SCALARS] * 3,
        out_specs=WHOLE,
        compiler_params=PARAMS,
        name="lists",
    )(measurement_tile_table, distance_damping, active_tile_tally)

    across, within = pl.pallas_call(
        pick_kernel,
        out_shape=(shape(2 * HANDED, OWN, OBS),) * 2,
        in_specs=[SCALARS, SCALARS, HBM, HBM, HBM],
        out_specs=(WHOLE, WHOLE),
        scratch_shapes=[
            pltpu.VMEM((HOME, OWN, OBS), BF16),
            pltpu.VMEM((HOME, 2, 128), F32),
            pltpu.VMEM((HOME, 2, 128), F32),
            pltpu.SemaphoreType.DMA((3,)),
        ],
        compiler_params=PARAMS,
        name="pick",
    )(region, edge_tile_handoff, blocks, val, wgt)
    across = swapped(across, 1)
    within = swapped(within, 0)

    def chain(split, fields, blocks, *about):
        _, region, *_, across, within = about
        share = []
        for count in split:
            start = sum(len(levels) for levels in share)
            share.append(tuple(range(start, start + count)))
        scratch = [
            pltpu.VMEM((PEERS, 2, 8, 256), BF16),
            pltpu.SemaphoreType.DMA((LEVELS + 1,)),
        ]
        packed = pl.pallas_call(
            functools.partial(pack_kernel, share[0]),
            out_shape=shape(PEERS, len(share[0]) + 2, OWN, COLS),
            in_specs=[SCALARS, HBM, HBM, WHOLE, WHOLE],
            out_specs=ANY,
            scratch_shapes=[
                pltpu.VMEM((HANDED, 2, OWN, COLS), BF16),
                pltpu.SemaphoreType.DMA((LEVELS + 2,)),
            ],
            compiler_params=PARAMS,
            name="pack",
        )(region, fields, blocks, across, within)
        gathered = exchange(packed)
        grams = pl.pallas_call(
            functools.partial(gram_kernel, share[1]),
            out_shape=shape(PEERS, len(share[1]) + 2, 8, 256),
            in_specs=[SCALARS] * 2 + [WHOLE] * 6 + [HBM],
            out_specs=ANY if share[1] else WHOLE,
            scratch_shapes=scratch,
            compiler_params=PARAMS,
            name="gram",
        )(*about, gathered, fields)
        entries = exchange(grams)
        come = [
            (levels, array)
            for levels, array in zip(share, (gathered, entries))
            if levels
        ]
        if not share[2]:
            earlier = [levels for levels, _ in come]
            sums, pert, centre = pl.pallas_call(
                functools.partial(combine_kernel, (), earlier),
                out_shape=(shape(PEERS, 2, 8, 256),) + CENTRED,
                in_specs=[WHOLE, HBM] + [WHOLE] * len(come),
                out_specs=(WHOLE,) * 3,
                scratch_shapes=scratch,
                compiler_params=PARAMS,
                name="combine",
            )(entries, fields, *(array for _, array in come))
            return pert, centre, exchange(sums)
        sums = pl.pallas_call(
            functools.partial(combine_kernel, share[2], ()),
            out_shape=shape(PEERS, len(share[2]) + 2, 8, 256),
            in_specs=[WHOLE, HBM],
            out_specs=ANY,
            scratch_shapes=scratch,
            compiler_params=PARAMS,
            name="combine",
        )(entries, fields)
        come.append((share[2], exchange(sums)))
        earlier = [levels for levels, _ in come]
        return pl.pallas_call(
            functools.partial(last_kernel, earlier),
            out_shape=CENTRED + (shape(PEERS, 2, 8, 256),),
            in_specs=[WHOLE] * len(come),
            out_specs=(WHOLE,) * 3,
            compiler_params=PARAMS,
            name="centre",
        )(*(array for _, array in come))

    even = lax.axis_index("region") % 2 == 0
    about = (me, region, lists, val, wgt, across, within)
    pert, centre, systems = lax.cond(
        even,
        functools.partial(chain, EVEN),
        functools.partial(chain, ODD),
        fields,
        blocks.reshape(HOME // 2, 2, OWN, OBS),
        *about,
    )

    mixed = pl.pallas_call(
        mix_kernel,
        out_shape=shape(PEERS, LEVELS, OWN, COLS),
        in_specs=[WHOLE] * 3,
        out_specs=WHOLE,
        compiler_params=PARAMS,
        name="mix",
    )(systems, pert, centre)
    analysis = pl.pallas_call(
        unpack_kernel,
        out_shape=shape(LEVELS, PEERS, OWN, COLS),
        in_specs=[ANY],
        out_specs=HBM,
        scratch_shapes=[pltpu.SemaphoreType.DMA((LEVELS,))],
        compiler_params=PARAMS,
        name="unpack",
    )(exchange(mixed))
    return analysis.transpose(2, 0, 1, 3).reshape(OWN, LEVELS, PEERS * COLS)


def solution(mesh):
    placed = (
        P("member", None, "region"),
        P("member", "region"),
        P("region"),
        P("region"),
        P(None, "region"),
        P(("region", "member"), None),
        P(("region", "member"), None),
        P(("region", "member")),
    )
    return jax.shard_map(
        on_device,
        mesh=mesh,
        in_specs=placed,
        out_specs=P("member", None, "region"),
        check_vma=False,
    )
```
